256 devices in a mesh: pts: 32 (over y, x, core), cam: 8 (over z).
Axes of the slice: x: 4, y: 4, z: 8, core: 2. Of those that a mesh axis runs over, the one named last changes fastest.
Arguments:
- jac_camera: bfloat16 [8, 18, 4, 4096], P('cam', None, None, 'pts'), may hold values from -4 to 4
- jac_point: bfloat16 [8, 6, 4, 4096], P('cam', None, None, 'pts'), may hold values from -6 to 6
- obs_camera: int32 [8, 4, 4096], P('cam', None, 'pts'), may hold values from 0 to 1023, as said below
- pair_groups: int32 [8, 2], P('cam'), may hold values from 0 to 7, as said below
- pair_points: int32 [8], P('cam'), may hold values from 512 to 4096, as said below
- damping: float32 [1], replicated, may hold values from 0.5 to 2
- rhs: float32 [8, 9, 128], replicated, may hold values from -6 to 6
Outputs:
- tiles: float32 [8, 2304, 2304], P('cam', 'pts')
- solution: float32 [8, 9, 128], replicated
The draws below stay inside these ranges and needn't reach their ends.
Inputs may be any that keep to these rules, and one draw needn't show every extreme that they name: `pair_groups`: each pair names two different groups, and every group lies in exactly two pairs. `obs_camera`: the 4 cameras of a point are different and lie in the two groups of the point's pair. `pair_points`: slots at or beyond this count are padding; at least one pair is full in every draw.
All inputs are finite; a program needn't handle non-finite values.
Results may differ from the reference program's by a relative error of at most 0.0013.
Values may be sent and summed in bfloat16 or wider, within the bound.
A program may use at most 128 MiB of HBM per device.

```python
import math
import jax
import jax.numpy as jnp
from jax import lax

GROUP = 128
TRACK = 4
ITERS = 2
PTS_PAIR = 4096
PAIRS = 8
GROUPS = 8


def pair_table(key):
    ordering = jax.random.permutation(jax.random.fold_in(key, 11), GROUPS)
    shuffle = jax.random.permutation(jax.random.fold_in(key, 12), PAIRS)
    return jnp.stack([ordering[shuffle], ordering[(shuffle + 1) % GROUPS]], axis=1).astype(jnp.int32)


def draw_pair_groups(key, part):
    return pair_table(key)


def draw_obs_camera(key, part):
    table = pair_table(key)
    scores = jax.random.randint(jax.random.fold_in(key, 13), (PAIRS, PTS_PAIR, 2 * GROUP), 0, 1 << 20)
    scores = scores * (2 * GROUP) + jnp.arange(2 * GROUP, dtype=jnp.int32)
    chosen = lax.top_k(scores, TRACK)[1].astype(jnp.int32)
    first_group = table[:, 0][:, None, None]
    second_group = table[:, 1][:, None, None]
    cameras = jnp.where(chosen < GROUP, first_group * GROUP + chosen, second_group * GROUP + chosen - GROUP)
    return jnp.transpose(cameras, (0, 2, 1)).astype(jnp.int32)


def draw_pair_points(key, part):
    counts = jax.random.randint(jax.random.fold_in(key, 14), (PAIRS,), PTS_PAIR // 8, PTS_PAIR // 2 + 1)
    busiest = jax.random.randint(jax.random.fold_in(key, 15), (), 0, PAIRS)
    return jnp.where(jnp.arange(PAIRS) == busiest, PTS_PAIR, counts).astype(jnp.int32)


def block_scale(rng, shape, shards, low, high):
    def one(dim, shards_of):
        steps = jax.random.uniform(jax.random.fold_in(jax.random.fold_in(rng, 6), dim), (shards_of,), jnp.float32, low / len(shards), high / len(shards))
        return jnp.repeat(jnp.exp(steps), shape[dim] // shards_of).reshape((-1,) + (1,) * (len(shape) - dim - 1))

    level = one(*shards[0])
    for cut in shards[1:]:
        level = level * one(*cut)
    return level


def scatter_about(stream_key, extent, deviation, most, shards=(), held_as=jnp.bfloat16):
    values = deviation * jax.random.normal(stream_key, extent, jnp.float32)
    if shards:
        values = values * block_scale(stream_key, extent, shards, -0.22, 0.18)
    return jnp.clip(values, -most, most).astype(held_as)


def setup_inputs(seed: int = 0) -> dict:
    streams_of = jax.random.split(jax.random.key(seed), 8)
    return {
        "jac_camera": scatter_about(streams_of[0], (PAIRS, 18, TRACK, PTS_PAIR), 0.25, 4.0, ((0, 8), (3, 32))),
        "jac_point": scatter_about(streams_of[1], (PAIRS, 6, TRACK, PTS_PAIR), 1.0, 6.0, ((0, 8), (3, 32))),
        "obs_camera": draw_obs_camera(jax.random.fold_in(streams_of[7], 71), 0),
        "pair_groups": draw_pair_groups(jax.random.fold_in(streams_of[7], 71), 0),
        "pair_points": draw_pair_points(jax.random.fold_in(streams_of[7], 71), 0),
        "damping": jnp.clip(jnp.exp(jax.random.uniform(streams_of[5], (1,), jnp.float32, math.log(0.5), math.log(2.0))), 0.5, 2.0),
        "rhs": scatter_about(streams_of[6], (GROUPS, 9, GROUP), 1.0, 6.0, (), jnp.float32),
    }


HIGHEST_PRECISION = lax.Precision.HIGHEST


def cross_three(first, second):
    return jnp.stack([first[1] * second[2] - first[2] * second[1],
                      first[2] * second[0] - first[0] * second[2],
                      first[0] * second[1] - first[1] * second[0]])


def invert_three(matrix):
    columns = [cross_three(matrix[1], matrix[2]), cross_three(matrix[2], matrix[0]), cross_three(matrix[0], matrix[1])]
    determinant = jnp.sum(matrix[0] * columns[0], axis=0)
    return jnp.stack(columns, axis=1) / determinant


def point_terms(camera_jac, point_half, live, damping_value):
    tracks = camera_jac.shape[2]
    point_jac = point_half.astype(jnp.float32)
    normal_matrix = jnp.einsum('rjkn,rlkn->jln', point_half, point_half, preferred_element_type=jnp.float32)
    normal_matrix = normal_matrix + damping_value * jnp.eye(3, dtype=jnp.float32)[:, :, None]
    inverse = invert_three(normal_matrix)
    weighted = jnp.einsum('rjkn,jln->rkln', point_jac, inverse, precision=HIGHEST_PRECISION)
    projected = jnp.einsum('rkln,slmn->rksmn', weighted, point_jac, precision=HIGHEST_PRECISION)
    identity = jnp.eye(2, dtype=jnp.float32)[:, None, :, None] * jnp.eye(tracks, dtype=jnp.float32)[None, :, None, :]
    reduced = (identity[..., None] - projected) * live
    return jnp.einsum('rikn,rksmn->iksmn', camera_jac, reduced, precision=HIGHEST_PRECISION)


def pair_tile(cam_rows, pnt_rows, cameras, groups_pair, live_count, damping_value):
    tracks = cam_rows.shape[1]
    points = cam_rows.shape[2]
    camera_half = cam_rows.reshape(2, 9, tracks, points)
    camera_jac = camera_half.astype(jnp.float32)
    point_half = pnt_rows.reshape(2, 3, tracks, points)
    camera_slot = jnp.where(cameras // GROUP == groups_pair[1], GROUP, 0) + cameras % GROUP
    live = (jnp.arange(points, dtype=jnp.int32) < live_count).astype(jnp.float32)
    mixed = point_terms(camera_jac, point_half, live, damping_value)
    rounded = mixed.astype(jnp.bfloat16)
    blocks = jnp.einsum('iksmn,sjmn->kmijn', rounded, camera_half, preferred_element_type=jnp.float32)
    halves = camera_slot // GROUP
    within = camera_slot % GROUP
    params = jnp.arange(9, dtype=jnp.int32)
    index = halves[:, None, :] * (9 * GROUP) + params[None, :, None] * GROUP + within[:, None, :]
    row_index = index[:, None, :, None, :]
    col_index = index[None, :, None, :, :]
    row_index, col_index = jnp.broadcast_arrays(row_index, col_index)
    empty = jnp.zeros((18 * GROUP, 18 * GROUP), jnp.float32)
    return empty.at[row_index, col_index].add(blocks)


def reference(jac_camera, jac_point, obs_camera, pair_groups, pair_points, damping, rhs):
    damping_value = damping[0]

    def one_pair(items):
        return pair_tile(items[0], items[1], items[2], items[3], items[4], damping_value)

    tiles = lax.map(one_pair, (jac_camera, jac_point, obs_camera, pair_groups, pair_points))

    def apply_system(vector):
        result = damping_value * vector
        for which in range(PAIRS):
            first_group = pair_groups[which, 0]
            second_group = pair_groups[which, 1]
            tile_vec = jnp.concatenate([vector[first_group].reshape(-1), vector[second_group].reshape(-1)])
            image = jnp.dot(tiles[which], tile_vec, precision=HIGHEST_PRECISION).reshape(2, 9, GROUP)
            result = result.at[first_group].add(image[0]).at[second_group].add(image[1])
        return result

    diagonal = damping_value * jnp.ones_like(rhs)
    for which in range(PAIRS):
        pieces = jnp.diagonal(tiles[which]).reshape(2, 9, GROUP)
        diagonal = diagonal.at[pair_groups[which, 0]].add(pieces[0]).at[pair_groups[which, 1]].add(pieces[1])

    solution = jnp.zeros_like(rhs)
    residual = rhs
    precond = residual / diagonal
    direction = precond
    inner = jnp.sum(residual * precond)
    for step in range(ITERS):
        image = apply_system(direction)
        alpha = inner / jnp.sum(direction * image)
        solution = solution + alpha * direction
        residual = residual - alpha * image
        precond = residual / diagonal
        inner_next = jnp.sum(residual * precond)
        direction = precond + (inner_next / inner) * direction
        inner = inner_next
    return tiles, solution
```

```python
import functools
import jax
import jax.numpy as jnp
from jax import lax
from jax.experimental import pallas as pl
from jax.experimental.pallas import tpu as pltpu
from jax.sharding import PartitionSpec as P

F32 = jnp.float32
BF16 = jnp.bfloat16
ROWS = 112
XROWS = 104


def iota(shape, dim):
    return lax.broadcasted_iota(jnp.int32, shape, dim)


def sym(a, b):
    return (a, b) if a <= b else (b, a)


def point_blocks(x_ref, b_ref, b8_ref, dg_ref, slot_ref, damp, live, i_low, i_high):
    def load(q):
        return x_ref[pl.ds(q, 8, stride=XROWS), :]

    def rounded(value):
        return value.astype(BF16).astype(F32)

    for k in range(4):
        slot_ref[pl.ds(k * 8, 8), :] = jnp.where(live, load(96 + k), -1.0)
    jp = {(r, j, k): load(72 + (3 * r + j) * 4 + k) for r in range(2) for j in range(3) for k in range(4)}
    normal = {}
    for a in range(3):
        for b in range(a, 3):
            total = None
            for k in range(4):
                for r in range(2):
                    term = jp[r, a, k] * jp[r, b, k]
                    total = term if total is None else total + term
            normal[a, b] = total + damp if a == b else total
    n00, n01, n02 = normal[0, 0], normal[0, 1], normal[0, 2]
    n11, n12, n22 = normal[1, 1], normal[1, 2], normal[2, 2]
    c00 = n11 * n22 - n12 * n12
    c01 = n02 * n12 - n01 * n22
    c02 = n01 * n12 - n02 * n11
    c11 = n00 * n22 - n02 * n02
    c12 = n01 * n02 - n00 * n12
    c22 = n00 * n11 - n01 * n01
    scale = 1.0 / (n00 * c00 + n01 * c01 + n02 * c02)
    inv = {(0, 0): c00 * scale, (0, 1): c01 * scale, (0, 2): c02 * scale,
           (1, 1): c11 * scale, (1, 2): c12 * scale, (2, 2): c22 * scale}
    weighted = {}
    for k in range(4):
        for r in range(2):
            for l in range(3):
                weighted[r, k, l] = sum(jp[r, j, k] * inv[sym(j, l)] for j in range(1, 3)) + jp[r, 0, k] * inv[sym(0, l)]
    reduced = {}
    for a in range(8):
        for b in range(a, 8):
            k, r, m, s = a // 2, a % 2, b // 2, b % 2
            value = weighted[r, k, 0] * jp[s, 0, m] + weighted[r, k, 1] * jp[s, 1, m] + weighted[r, k, 2] * jp[s, 2, m]
            reduced[a, b] = 1.0 - value if a == b else -value

    def red(k, r, m, s):
        return reduced[sym(2 * k + r, 2 * m + s)]

    def camera(r, i, k):
        return load((9 * r + i) * 4 + k)

    for m in range(4):
        right = {(s, j): camera(s, j, m) for s in range(2) for j in range(9)}
        for j in range(9):
            parts = [
                rounded(right[0, j] * red(m, 0, m, s) + right[1, j] * red(m, 1, m, s)) * right[s, j]
                for s in range(2)
            ]
            dg_ref[pl.ds(m * 128 + j, 8, stride=16), :] = parts[0] + parts[1]
        for k in range(4):
            for which, i in enumerate((i_low, i_high)):
                left = [camera(r, i, k) for r in range(2)]
                mixed = [
                    rounded(left[0] * red(k, 0, m, s) + left[1] * red(k, 1, m, s)) for s in range(2)
                ]
                base = (which * 16 + k * 4 + m)
                for j in range(9):
                    value = mixed[0] * right[0, j] + mixed[1] * right[1, j]
                    if j < 8:
                        b_ref[pl.ds(base * 64 + j, 8, stride=8), :] = value
                    else:
                        b8_ref[pl.ds(base * 8, 8), :] = value


def twice(value):
    return jnp.concatenate([value, value], axis=0).astype(BF16)


def build_source(s, l_ref, r_ref, pb_ref, b_ref, b8_ref, dg_ref, slot_ref, target_ref, target8_ref, iota_ref, which_i):
    def row(ref, index):
        return jnp.broadcast_to(ref[pl.ds(index, 1), :], (8, 128))

    slots = [twice(row(slot_ref, k * 8 + s)) for k in range(4)]
    zero = jnp.zeros((16, 128), BF16)
    one = jnp.ones((16, 128), BF16)
    for b in range(16):
        value = iota_ref[pl.ds(b * 16, 16), :]
        for m in range(4):
            r_ref[pl.ds(b * 16, 16), pl.ds(m * 128, 128)] = jnp.where(slots[m] == value, one, zero)
    for which in range(2):
        for km in range(16):
            base = pl.multiple_of(((which * 16 + km) * 8 + s) * 8, 8)
            pb_ref[which, pl.ds(km * 16, 16), :] = twice(b_ref[pl.ds(base, 8), :])

    def choose(masks, values):
        value = zero
        for k in range(4):
            value = jnp.where(masks[k], values[k], value)
        return value

    for g in range(9):
        which = which_i[g]
        ops = [pb_ref[which, pl.ds(km * 16, 16), :] for km in range(16)]
        for b in range(4):
            first = (g * 4 + b) * 16
            target = target_ref[pl.ds(first, 16), :]
            masks = [slots[k] == target for k in range(4)]
            for m in range(4):
                l_ref[pl.ds(first, 16), pl.ds(m * 128, 128)] = choose(masks, [ops[k * 4 + m] for k in range(4)])
    for b in range(5):
        target = target8_ref[pl.ds(b * 16, 16), :]
        masks = [slots[k] == target for k in range(4)]
        low, high = which_i[2 * b], which_i[min(2 * b + 1, 8)]
        for m in range(4):
            values = []
            for k in range(4):
                km = k * 4 + m
                both = jnp.concatenate(
                    [row(b8_ref, (low * 16 + km) * 8 + s), row(b8_ref, (high * 16 + km) * 8 + s)], axis=0
                )
                values.append(both.astype(BF16))
            l_ref[pl.ds(576 + b * 16, 16), pl.ds(m * 128, 128)] = choose(masks, values)
    for m in range(4):
        base = pl.multiple_of((m * 8 + s) * 16, 16)
        l_ref[pl.ds(656, 16), pl.ds(m * 128, 128)] = dg_ref[pl.ds(base, 16), :].astype(BF16)


def place(position):
    first_row = position * 72
    half = position // 16
    inside = first_row - half * 1152
    i_low = inside // 128
    start = inside - i_low * 128
    i_high = jnp.minimum(i_low + 1, 8)
    which_i = [(start + 8 * g) // 128 for g in range(9)]
    return half, start, i_low, i_high, which_i


def prepare(position, target_ref, target8_ref, iota_ref, dg_ref):
    half, start, _, _, _ = place(position)

    def slot_of(r):
        return half * 128 + (start + r) % 128

    target_ref[...] = slot_of(iota((576, 128), 0) // 8).astype(F32).astype(BF16)
    row8 = iota((80, 128), 0)
    target8_ref[...] = jnp.where(row8 < 72, slot_of(row8), -2).astype(F32).astype(BF16)
    iota_ref[...] = iota((256, 128), 0).astype(F32).astype(BF16)
    dg_ref[...] = jnp.zeros_like(dg_ref)


def group_work(group, read_chunk, count, damp, position, out_acc, scr, first):
    (x_ref, b_ref, b8_ref, dg_ref, slot_ref, l_ref, r_ref, pb_ref, target_ref, target8_ref, iota_ref) = scr
    _, _, i_low, i_high, which_i = place(position)

    def widen(s, carry):
        x_ref[pl.ds(pl.multiple_of(s * XROWS, 8), XROWS), :] = read_chunk(group * 8 + s)[:XROWS].astype(F32)
        return carry

    lax.fori_loop(0, 8, widen, 0)
    index = (group * 8 + iota((8, 128), 0)) * 128 + iota((8, 128), 1)
    point_blocks(x_ref, b_ref, b8_ref, dg_ref, slot_ref, damp, index < count, i_low, i_high)

    def build(s, slot):
        build_source(s, l_ref.at[slot], r_ref.at[slot], pb_ref.at[slot], b_ref, b8_ref, dg_ref, slot_ref, target_ref, target8_ref, iota_ref, which_i)

    def product(slot):
        value = lax.dot_general(l_ref[slot], r_ref[slot], (((1,), (1,)), ((), ())), preferred_element_type=F32)
        out_acc[0] += value[:, :128]
        out_acc[1] += value[:, 128:]

    build(0, 0)

    def pair(t, carry):
        build(2 * t + 1, 1)
        product(0)
        build(jnp.minimum(2 * t + 2, 7), 0)
        product(1)
        return carry

    lax.fori_loop(0, 4, pair, 0)


def scratch():
    return [
        pltpu.VMEM((8 * XROWS, 128), F32),
        pltpu.VMEM((2 * 16 * 64, 128), F32),
        pltpu.VMEM((2 * 16 * 8, 128), F32),
        pltpu.VMEM((4 * 8 * 16, 128), F32),
        pltpu.VMEM((4 * 8, 128), F32),
        pltpu.VMEM((2, 672, 512), BF16),
        pltpu.VMEM((2, 256, 512), BF16),
        pltpu.VMEM((2, 2, 256, 128), BF16),
        pltpu.VMEM((576, 128), BF16),
        pltpu.VMEM((80, 128), BF16),
        pltpu.VMEM((256, 128), BF16),
    ]


def unpack_tile(acc_ref, tile_ref):
    for g in range(9):
        for h in range(2):
            for j in range(8):
                tile_ref[pl.ds(g * 8, 8), pl.ds(h * 1152 + j * 128, 128)] = acc_ref[h, pl.ds(g * 64 + j, 8, stride=8), :]
            tile_ref[pl.ds(g * 8, 8), pl.ds(h * 1152 + 1024, 128)] = acc_ref[h, pl.ds(576 + g * 8, 8), :]


def tile_kernel(count_ref, damp_ref, gather_ref, tile_ref, diag_ref, acc_ref, *scr):
    position = lax.axis_index("pts")
    prepare(position, scr[8], scr[9], scr[10], scr[3])
    acc_ref[...] = jnp.zeros_like(acc_ref)

    def loop(group, carry):
        group_work(group, lambda s: gather_ref[s], count_ref[0], damp_ref[0], position, acc_ref, scr, False)
        return carry

    lax.fori_loop(0, 4, loop, 0)
    unpack_tile(acc_ref, tile_ref)
    for h in range(2):
        diag_ref[h] = acc_ref[h, pl.ds(656, 16), :]


def tile_call(count, damp, gathered):
    vm = pl.BlockSpec(memory_space=pltpu.VMEM)
    sm = pl.BlockSpec(memory_space=pltpu.SMEM)
    return pl.pallas_call(
        tile_kernel,
        out_shape=(jax.ShapeDtypeStruct((72, 2304), F32), jax.ShapeDtypeStruct((2, 16, 128), F32)),
        in_specs=[sm, sm, vm],
        out_specs=(vm, vm),
        scratch_shapes=[pltpu.VMEM((2, 672, 128), F32)] + scratch(),
        compiler_params=pltpu.CompilerParams(vmem_limit_bytes=40 * 2**20),
        name="tile_rows",
    )(count, damp, gathered)


def body(jac_camera, jac_point, obs_camera, pair_groups, pair_points, damping, rhs):
    first, second = pair_groups[0, 0], pair_groups[0, 1]
    cameras = obs_camera[0]
    slot = jnp.where(cameras // 128 == second, 128, 0) + cameras % 128
    packed = jnp.concatenate(
        [jac_camera[0].reshape(72, 128), jac_point[0].reshape(24, 128), slot.astype(BF16), jnp.zeros((12, 128), BF16)], axis=0
    )
    gathered = lax.all_gather(packed, "pts", axis=0, tiled=False)
    tile, diag = tile_call(pair_points, damping, gathered)
    diag = diag[:, :9]
    d = damping[0]
    fh = (jnp.arange(8) == first).astype(F32)[:, None, None]
    sh = (jnp.arange(8) == second).astype(F32)[:, None, None]
    diagonal = lax.psum(fh * diag[0] + sh * diag[1], "cam") + d
    position = lax.axis_index("pts")

    def tvec(v):
        return jnp.concatenate([v[first].reshape(-1), v[second].reshape(-1)])

    z = rhs / diagonal
    p = z
    rz = jnp.sum(rhs * z)
    y = jnp.sum(tile * tvec(p)[None, :], axis=1)
    whole = lax.dynamic_update_slice_in_dim(jnp.zeros((2304,), F32), y, position * 72, 0).reshape(2, 9, 128)
    q = lax.psum(fh * whole[0] + sh * whole[1], ("pts", "cam")) + d * p
    alpha = rz / jnp.sum(p * q)
    x = alpha * p
    r = rhs - alpha * q
    z = r / diagonal
    new = jnp.sum(r * z)
    p = z + (new / rz) * p
    tv = tvec(p)
    y = jnp.sum(tile * tv[None, :], axis=1)
    own = lax.dynamic_slice_in_dim(tv, position * 72, 72, 0)
    pq = lax.psum(jnp.sum(own * y), ("pts", "cam")) + d * jnp.sum(p * p)
    x = x + (new / pq) * p
    return tile[None], x


def solution(mesh):
    placed = (P("cam", None, None, "pts"), P("cam", None, None, "pts"), P("cam", None, "pts"), P("cam", None), P("cam"), P(), P())
    return jax.shard_map(body, mesh=mesh, in_specs=placed, out_specs=(P("cam", "pts", None), P()), check_vma=False)
```

```python
import functools
import jax
import jax.numpy as jnp
from jax import lax
from jax.experimental import pallas as pl
from jax.experimental.pallas import tpu as pltpu
from jax.sharding import PartitionSpec as P

F32 = jnp.float32
BF16 = jnp.bfloat16
ROWS = 112
XROWS = 104


def iota(shape, dim):
    return lax.broadcasted_iota(jnp.int32, shape, dim)


def sym(a, b):
    return (a, b) if a <= b else (b, a)


def point_blocks(x_ref, b_ref, b8_ref, dg_ref, slot_ref, damp, live, i_low, i_high):
    def load(q):
        return x_ref[pl.ds(q, 8, stride=XROWS), :]

    def rounded(value):
        return value.astype(BF16).astype(F32)

    for k in range(4):
        slot_ref[pl.ds(k * 8, 8), :] = jnp.where(live, load(96 + k), -1.0)
    jp = {(r, j, k): load(72 + (3 * r + j) * 4 + k) for r in range(2) for j in range(3) for k in range(4)}
    normal = {}
    for a in range(3):
        for b in range(a, 3):
            total = None
            for k in range(4):
                for r in range(2):
                    term = jp[r, a, k] * jp[r, b, k]
                    total = term if total is None else total + term
            normal[a, b] = total + damp if a == b else total
    n00, n01, n02 = normal[0, 0], normal[0, 1], normal[0, 2]
    n11, n12, n22 = normal[1, 1], normal[1, 2], normal[2, 2]
    c00 = n11 * n22 - n12 * n12
    c01 = n02 * n12 - n01 * n22
    c02 = n01 * n12 - n02 * n11
    c11 = n00 * n22 - n02 * n02
    c12 = n01 * n02 - n00 * n12
    c22 = n00 * n11 - n01 * n01
    scale = 1.0 / (n00 * c00 + n01 * c01 + n02 * c02)
    inv = {(0, 0): c00 * scale, (0, 1): c01 * scale, (0, 2): c02 * scale,
           (1, 1): c11 * scale, (1, 2): c12 * scale, (2, 2): c22 * scale}
    weighted = {}
    for k in range(4):
        for r in range(2):
            for l in range(3):
                weighted[r, k, l] = sum(jp[r, j, k] * inv[sym(j, l)] for j in range(1, 3)) + jp[r, 0, k] * inv[sym(0, l)]
    reduced = {}
    for a in range(8):
        for b in range(a, 8):
            k, r, m, s = a // 2, a % 2, b // 2, b % 2
            value = weighted[r, k, 0] * jp[s, 0, m] + weighted[r, k, 1] * jp[s, 1, m] + weighted[r, k, 2] * jp[s, 2, m]
            reduced[a, b] = 1.0 - value if a == b else -value

    def red(k, r, m, s):
        return reduced[sym(2 * k + r, 2 * m + s)]

    def camera(r, i, k):
        return load((9 * r + i) * 4 + k)

    for m in range(4):
        right = {(s, j): camera(s, j, m) for s in range(2) for j in range(9)}
        for j in range(9):
            parts = [
                rounded(right[0, j] * red(m, 0, m, s) + right[1, j] * red(m, 1, m, s)) * right[s, j]
                for s in range(2)
            ]
            dg_ref[pl.ds(m * 128 + j, 8, stride=16), :] = parts[0] + parts[1]
        for k in range(4):
            for which, i in enumerate((i_low, i_high)):
                left = [camera(r, i, k) for r in range(2)]
                mixed = [
                    rounded(left[0] * red(k, 0, m, s) + left[1] * red(k, 1, m, s)) for s in range(2)
                ]
                base = (which * 16 + k * 4 + m)
                for j in range(9):
                    value = mixed[0] * right[0, j] + mixed[1] * right[1, j]
                    if j < 8:
                        b_ref[pl.ds(base * 64 + j, 8, stride=8), :] = value
                    else:
                        b8_ref[pl.ds(base * 8, 8), :] = value


def twice(value):
    return jnp.concatenate([value, value], axis=0).astype(BF16)


def build_source(s, l_ref, r_ref, pb_ref, b_ref, b8_ref, dg_ref, slot_ref, target_ref, target8_ref, iota_ref, which_i):
    def row(ref, index):
        return jnp.broadcast_to(ref[pl.ds(index, 1), :], (8, 128))

    slots = [twice(row(slot_ref, k * 8 + s)) for k in range(4)]
    zero = jnp.zeros((16, 128), BF16)
    one = jnp.ones((16, 128), BF16)
    for b in range(16):
        value = iota_ref[pl.ds(b * 16, 16), :]
        for m in range(4):
            r_ref[pl.ds(b * 16, 16), pl.ds(m * 128, 128)] = jnp.where(slots[m] == value, one, zero)
    for which in range(2):
        for km in range(16):
            base = pl.multiple_of(((which * 16 + km) * 8 + s) * 8, 8)
            pb_ref[which, pl.ds(km * 16, 16), :] = twice(b_ref[pl.ds(base, 8), :])

    def choose(masks, values):
        value = zero
        for k in range(4):
            value = jnp.where(masks[k], values[k], value)
        return value

    for g in range(9):
        which = which_i[g]
        ops = [pb_ref[which, pl.ds(km * 16, 16), :] for km in range(16)]
        for b in range(4):
            first = (g * 4 + b) * 16
            target = target_ref[pl.ds(first, 16), :]
            masks = [slots[k] == target for k in range(4)]
            for m in range(4):
                l_ref[pl.ds(first, 16), pl.ds(m * 128, 128)] = choose(masks, [ops[k * 4 + m] for k in range(4)])
    for b in range(5):
        target = target8_ref[pl.ds(b * 16, 16), :]
        masks = [slots[k] == target for k in range(4)]
        low, high = which_i[2 * b], which_i[min(2 * b + 1, 8)]
        for m in range(4):
            values = []
            for k in range(4):
                km = k * 4 + m
                both = jnp.concatenate(
                    [row(b8_ref, (low * 16 + km) * 8 + s), row(b8_ref, (high * 16 + km) * 8 + s)], axis=0
                )
                values.append(both.astype(BF16))
            l_ref[pl.ds(576 + b * 16, 16), pl.ds(m * 128, 128)] = choose(masks, values)
    for m in range(4):
        base = pl.multiple_of((m * 8 + s) * 16, 16)
        l_ref[pl.ds(656, 16), pl.ds(m * 128, 128)] = dg_ref[pl.ds(base, 16), :].astype(BF16)


def place(position):
    first_row = position * 72
    half = position // 16
    inside = first_row - half * 1152
    i_low = inside // 128
    start = inside - i_low * 128
    i_high = jnp.minimum(i_low + 1, 8)
    which_i = [(start + 8 * g) // 128 for g in range(9)]
    return half, start, i_low, i_high, which_i


def prepare(position, target_ref, target8_ref, iota_ref, dg_ref):
    half, start, _, _, _ = place(position)

    def slot_of(r):
        return half * 128 + (start + r) % 128

    target_ref[...] = slot_of(iota((576, 128), 0) // 8).astype(F32).astype(BF16)
    row8 = iota((80, 128), 0)
    target8_ref[...] = jnp.where(row8 < 72, slot_of(row8), -2).astype(F32).astype(BF16)
    iota_ref[...] = iota((256, 128), 0).astype(F32).astype(BF16)
    dg_ref[...] = jnp.zeros_like(dg_ref)


def group_work(group, read_chunk, count, damp, position, out_acc, scr, first):
    (x_ref, b_ref, b8_ref, dg_ref, slot_ref, l_ref, r_ref, pb_ref, target_ref, target8_ref, iota_ref) = scr
    _, _, i_low, i_high, which_i = place(position)

    def widen(s, carry):
        x_ref[pl.ds(pl.multiple_of(s * XROWS, 8), XROWS), :] = read_chunk(group * 8 + s)[:XROWS].astype(F32)
        return carry

    lax.fori_loop(0, 8, widen, 0)
    index = (group * 8 + iota((8, 128), 0)) * 128 + iota((8, 128), 1)
    point_blocks(x_ref, b_ref, b8_ref, dg_ref, slot_ref, damp, index < count, i_low, i_high)

    def build(s, slot):
        build_source(s, l_ref.at[slot], r_ref.at[slot], pb_ref.at[slot], b_ref, b8_ref, dg_ref, slot_ref, target_ref, target8_ref, iota_ref, which_i)

    def product(slot):
        value = lax.dot_general(l_ref[slot], r_ref[slot], (((1,), (1,)), ((), ())), preferred_element_type=F32)
        out_acc[0] += value[:, :128]
        out_acc[1] += value[:, 128:]

    build(0, 0)

    def pair(t, carry):
        build(2 * t + 1, 1)
        product(0)
        build(jnp.minimum(2 * t + 2, 7), 0)
        product(1)
        return carry

    lax.fori_loop(0, 4, pair, 0)


def scratch():
    return [
        pltpu.VMEM((8 * XROWS, 128), F32),
        pltpu.VMEM((2 * 16 * 64, 128), F32),
        pltpu.VMEM((2 * 16 * 8, 128), F32),
        pltpu.VMEM((4 * 8 * 16, 128), F32),
        pltpu.VMEM((4 * 8, 128), F32),
        pltpu.VMEM((2, 672, 512), BF16),
        pltpu.VMEM((2, 256, 512), BF16),
        pltpu.VMEM((2, 2, 256, 128), BF16),
        pltpu.VMEM((576, 128), BF16),
        pltpu.VMEM((80, 128), BF16),
        pltpu.VMEM((256, 128), BF16),
    ]


def unpack_tile(acc_ref, tile_ref):
    for g in range(9):
        for h in range(2):
            for j in range(8):
                tile_ref[pl.ds(g * 8, 8), pl.ds(h * 1152 + j * 128, 128)] = acc_ref[h, pl.ds(g * 64 + j, 8, stride=8), :]
            tile_ref[pl.ds(g * 8, 8), pl.ds(h * 1152 + 1024, 128)] = acc_ref[h, pl.ds(576 + g * 8, 8), :]


def tile_kernel(count_ref, damp_ref, gather_ref, tile_ref, diag_ref, acc_ref, *scr):
    position = lax.axis_index("pts")
    prepare(position, scr[8], scr[9], scr[10], scr[3])
    acc_ref[...] = jnp.zeros_like(acc_ref)

    def loop(group, carry):
        group_work(group, lambda s: gather_ref[s], count_ref[0], damp_ref[0], position, acc_ref, scr, False)
        return carry

    lax.fori_loop(0, 4, loop, 0)
    unpack_tile(acc_ref, tile_ref)
    for h in range(2):
        diag_ref[h] = acc_ref[h, pl.ds(656, 16), :]


def tile_call(count, damp, gathered):
    vm = pl.BlockSpec(memory_space=pltpu.VMEM)
    sm = pl.BlockSpec(memory_space=pltpu.SMEM)
    return pl.pallas_call(
        tile_kernel,
        out_shape=(jax.ShapeDtypeStruct((72, 2304), F32), jax.ShapeDtypeStruct((2, 16, 128), F32)),
        in_specs=[sm, sm, vm],
        out_specs=(vm, vm),
        scratch_shapes=[pltpu.VMEM((2, 672, 128), F32)] + scratch(),
        compiler_params=pltpu.CompilerParams(vmem_limit_bytes=40 * 2**20),
        name="tile_rows",
    )(count, damp, gathered)


MESH = pl.DeviceIdType.MESH
PTS = 32
CAM = 8


def here():
    return lax.axis_index("pts"), lax.axis_index("cam")


def plane_peer(d):
    pts, cam = here()
    return (pts + d) % PTS, cam


def line_peer(d):
    pts, cam = here()
    return pts, (cam + d) % CAM


def greet(plane, line):
    barrier = pltpu.get_barrier_semaphore()
    if plane:
        def one(d, carry):
            pl.semaphore_signal(barrier, inc=1, device_id=plane_peer(d), device_id_type=MESH)
            return carry

        lax.fori_loop(1, PTS, one, 0)
    if line:
        for d in range(1, CAM):
            pl.semaphore_signal(barrier, inc=1, device_id=line_peer(d), device_id_type=MESH)


def greeted(plane, line):
    pl.semaphore_wait(pltpu.get_barrier_semaphore(), (PTS - 1 if plane else 0) + (CAM - 1 if line else 0))


class Exchange:
    def __init__(self, plane, block, send_sem, recv_sem):
        self.size = PTS if plane else CAM
        self.peer = plane_peer if plane else line_peer
        self.me = here()[0 if plane else 1]
        self.block, self.send_sem, self.recv_sem = block, send_sem, recv_sem

    def copy(self, d):
        return pltpu.make_async_remote_copy(
            src_ref=self.block(self.me),
            dst_ref=self.block(self.me),
            send_sem=self.send_sem.at[d],
            recv_sem=self.recv_sem.at[self.me],
            device_id=self.peer(d),
            device_id_type=MESH,
        )

    def arrival(self, d):
        other = (self.me + d) % self.size
        return pltpu.make_async_remote_copy(
            src_ref=self.block(other),
            dst_ref=self.block(other),
            send_sem=self.send_sem.at[d],
            recv_sem=self.recv_sem.at[other],
            device_id=self.peer(d),
            device_id_type=MESH,
        )

    def each(self, action):
        def one(d, carry):
            action(d)
            return carry

        lax.fori_loop(1, self.size, one, 0)

    def send(self):
        self.each(lambda d: self.copy(d).start())

    def receive(self):
        self.each(lambda d: self.arrival(d).wait_recv())

    def sent(self):
        self.each(lambda d: self.copy(d).wait_send())


def pos_place(position):
    first_row = position * 72
    half = position // 16
    inside = first_row % 1152
    return half, inside // 128, inside % 128


def spread(ref, index):
    return jnp.broadcast_to(ref[pl.ds(index, 1), :], (8, 128))


def total_of(values):
    total = values[0]
    for value in values[1:]:
        total = total + value
    return jnp.sum(jnp.sum(total, axis=0, keepdims=True), axis=1, keepdims=True)


def solve(tile_ref, diag_block, groups_ref, damp, rhs_ref, out_ref, zd_ref, v_ref, zq_ref, pq_ref, zs_ref, ps_ref, sems):
    position, cam = here()
    half, start, i_low, i_high, which_i = place(position)
    group_of = [groups_ref[0, 0], groups_ref[0, 1]]
    sub = iota((8, 128), 0)
    lane = iota((8, 128), 1)
    subf = sub.astype(F32)
    for h in range(2):
        tagged = jnp.where(iota((16, 128), 0) == 9, group_of[h].astype(F32), diag_block(h))
        zd_ref[pl.ds(pl.multiple_of((cam * 2 + h) * 16, 16), 16), :] = tagged
    zd = Exchange(False, lambda t: zd_ref.at[pl.ds(pl.multiple_of(t * 32, 32), 32), :], sems[0], sems[1])
    zd.send()
    zd.receive()
    member = {(t, h): spread(zd_ref, (t * 2 + h) * 16 + 9) == subf for t in range(CAM) for h in range(2)}
    residual = [rhs_ref[i] for i in range(9)]
    diagonal = []
    for i in range(9):
        total = jnp.full((8, 128), damp, F32)
        for t in range(CAM):
            for h in range(2):
                total = total + jnp.where(member[t, h], spread(zd_ref, (t * 2 + h) * 16 + i), 0.0)
        diagonal.append(total)
    precond = [residual[i] / diagonal[i] for i in range(9)]
    inner = total_of([residual[i] * precond[i] for i in range(9)])
    own_member = [spread(zd_ref, (t * 2 + half) * 16 + 9) == subf for t in range(CAM)]

    def image_row(vector):
        for i in range(9):
            v_ref[pl.ds(i * 8, 8), :] = vector[i]
        ops = [[spread(v_ref, j * 8 + group_of[h]) for j in range(9)] for h in range(2)]
        placed = jnp.zeros((8, 128), F32)
        for g in range(9):
            total = None
            for h in range(2):
                for j in range(9):
                    term = tile_ref[pl.ds(g * 8, 8), pl.ds((h * 9 + j) * 128, 128)] * ops[h][j]
                    total = term if total is None else total + term
            value = jnp.sum(total, axis=1, keepdims=True)
            placed = placed + jnp.where(lane == (start + 8 * g + sub) % 128, value, 0.0)
        return jnp.sum(placed, axis=0, keepdims=True)

    zq_ref[pl.ds(cam, 1), :] = image_row(precond)
    zq = Exchange(False, lambda t: zq_ref.at[pl.ds(t, 1), :], sems[2], sems[3])
    zq.send()
    zq.receive()
    total = jnp.zeros((8, 128), F32)
    for t in range(CAM):
        total = total + jnp.where(own_member[t], spread(zq_ref, t), 0.0)
    pq_ref[pl.ds(pl.multiple_of(position * 8, 8), 8), :] = total
    pq = Exchange(True, lambda p: pq_ref.at[pl.ds(pl.multiple_of(p * 8, 8), 8), :], sems[4], sems[5])
    pq.send()
    pq.receive()
    image = [damp * precond[i] for i in range(9)]
    for p in range(PTS):
        _, low, first = pos_place(p)
        value = pq_ref[pl.ds(p * 8, 8), :]
        if first + 72 > 128:
            image[low] = image[low] + jnp.where(lane >= first, value, 0.0)
            image[low + 1] = image[low + 1] + jnp.where(lane >= first, 0.0, value)
        else:
            image[low] = image[low] + value
    alpha = inner / total_of([precond[i] * image[i] for i in range(9)])
    residual = [residual[i] - alpha * image[i] for i in range(9)]
    scaled = [residual[i] / diagonal[i] for i in range(9)]
    inner_next = total_of([residual[i] * scaled[i] for i in range(9)])
    beta = inner_next / inner
    direction = [scaled[i] + beta * precond[i] for i in range(9)]
    row = image_row(direction)
    own_group = jnp.where(half == 0, group_of[0], group_of[1])
    lane_row = iota((1, 128), 1)
    own = jnp.where(
        lane_row >= start, v_ref[pl.ds(i_low * 8 + own_group, 1), :], v_ref[pl.ds(i_high * 8 + own_group, 1), :]
    )
    zs_ref[pl.ds(cam, 1), :] = row * own
    zs = Exchange(False, lambda t: zs_ref.at[pl.ds(t, 1), :], sems[6], sems[7])
    zs.send()
    zs.receive()
    ps_ref[pl.ds(position, 1), :] = jnp.sum(zs_ref[...], axis=0, keepdims=True)
    ps = Exchange(True, lambda p: ps_ref.at[pl.ds(p, 1), :], sems[8], sems[9])
    ps.send()
    ps.receive()
    curvature = damp * total_of([value * value for value in direction]) + total_of(
        [ps_ref[pl.ds(8 * n, 8), :] for n in range(4)]
    )
    second = inner_next / curvature
    for i in range(9):
        out_ref[i] = alpha * precond[i] + second * direction[i]
    for exchange in (zd, zq, pq, zs, ps):
        exchange.sent()


def solve_scratch():
    return [
        pltpu.VMEM((CAM * 32, 128), F32),
        pltpu.VMEM((72, 128), F32),
        pltpu.VMEM((CAM, 128), F32),
        pltpu.VMEM((PTS * 8, 128), F32),
        pltpu.VMEM((CAM, 128), F32),
        pltpu.VMEM((PTS, 128), F32),
    ]


def solve_sems():
    return [pltpu.SemaphoreType.DMA((n,)) for n in (CAM, CAM, CAM, CAM, PTS, PTS, CAM, CAM, PTS, PTS)]


def gather_kernel(packed_ref, out_ref, send_sem, recv_sem):
    position, _ = here()
    greet(True, False)
    out_ref[position] = packed_ref[...]
    greeted(True, False)
    chunks = Exchange(True, lambda p: out_ref.at[p], send_sem, recv_sem)
    chunks.send()
    chunks.receive()
    chunks.sent()


def solve_kernel(groups_ref, damp_ref, tile_ref, diag_ref, rhs_ref, out_ref, *scr):
    greet(True, True)
    greeted(True, True)
    solve(tile_ref, lambda h: diag_ref[h], groups_ref, damp_ref[0], rhs_ref, out_ref, *scr[:6], scr[6:])


def body(jac_camera, jac_point, obs_camera, pair_groups, pair_points, damping, rhs):
    second = pair_groups[0, 1]
    cameras = obs_camera[0]
    slot = jnp.where(cameras // 128 == second, 128, 0) + cameras % 128
    packed = jnp.concatenate(
        [jac_camera[0].reshape(72, 128), jac_point[0].reshape(24, 128), slot.astype(BF16), jnp.zeros((12, 128), BF16)], axis=0
    )
    vm = pl.BlockSpec(memory_space=pltpu.VMEM)
    sm = pl.BlockSpec(memory_space=pltpu.SMEM)
    gathered = pl.pallas_call(
        gather_kernel,
        out_shape=jax.ShapeDtypeStruct((PTS, ROWS, 128), BF16),
        in_specs=[vm],
        out_specs=vm,
        scratch_shapes=[pltpu.SemaphoreType.DMA((PTS,)), pltpu.SemaphoreType.DMA((PTS,))],
        compiler_params=pltpu.CompilerParams(collective_id=0, has_side_effects=True, vmem_limit_bytes=16 * 2**20),
        name="gather_points",
    )(packed)
    tile, diag = tile_call(pair_points, damping, gathered)
    solved = pl.pallas_call(
        solve_kernel,
        out_shape=jax.ShapeDtypeStruct((9, 8, 128), F32),
        in_specs=[sm, sm, vm, vm, vm],
        out_specs=vm,
        scratch_shapes=solve_scratch() + solve_sems(),
        compiler_params=pltpu.CompilerParams(collective_id=1, has_side_effects=True, vmem_limit_bytes=16 * 2**20),
        name="solve_system",
    )(pair_groups, damping, tile, diag, rhs.transpose(1, 0, 2))
    return tile[None], solved.transpose(1, 0, 2)


def solution(mesh):
    placed = (P("cam", None, None, "pts"), P("cam", None, None, "pts"), P("cam", None, "pts"), P("cam", None), P("cam"), P(), P())
    return jax.shard_map(body, mesh=mesh, in_specs=placed, out_specs=(P("cam", "pts", None), P()), check_vma=False)
```

```python
import functools
import jax
import jax.numpy as jnp
from jax import lax
from jax.experimental import pallas as pl
from jax.experimental.pallas import tpu as pltpu
from jax.sharding import PartitionSpec as P

F32 = jnp.float32
BF16 = jnp.bfloat16
ROWS = 112
XROWS = 104
UNROLL = 4


def iota(shape, dim):
    return lax.broadcasted_iota(jnp.int32, shape, dim)


def sym(a, b):
    return (a, b) if a <= b else (b, a)


def point_blocks(x_ref, b_ref, b8_ref, dg_ref, slot_ref, damp, live, i_low, i_high):
    def load(q):
        return x_ref[pl.ds(q, 8, stride=XROWS), :]

    def rounded(value):
        return value.astype(BF16).astype(F32)

    for k in range(4):
        slot_ref[pl.ds(k * 8, 8), :] = jnp.where(live, load(96 + k), -1.0)
    jp = {(r, j, k): load(72 + (3 * r + j) * 4 + k) for r in range(2) for j in range(3) for k in range(4)}
    normal = {}
    for a in range(3):
        for b in range(a, 3):
            total = None
            for k in range(4):
                for r in range(2):
                    term = jp[r, a, k] * jp[r, b, k]
                    total = term if total is None else total + term
            normal[a, b] = total + damp if a == b else total
    n00, n01, n02 = normal[0, 0], normal[0, 1], normal[0, 2]
    n11, n12, n22 = normal[1, 1], normal[1, 2], normal[2, 2]
    c00 = n11 * n22 - n12 * n12
    c01 = n02 * n12 - n01 * n22
    c02 = n01 * n12 - n02 * n11
    c11 = n00 * n22 - n02 * n02
    c12 = n01 * n02 - n00 * n12
    c22 = n00 * n11 - n01 * n01
    scale = 1.0 / (n00 * c00 + n01 * c01 + n02 * c02)
    inv = {(0, 0): c00 * scale, (0, 1): c01 * scale, (0, 2): c02 * scale,
           (1, 1): c11 * scale, (1, 2): c12 * scale, (2, 2): c22 * scale}
    weighted = {}
    for k in range(4):
        for r in range(2):
            for l in range(3):
                weighted[r, k, l] = sum(jp[r, j, k] * inv[sym(j, l)] for j in range(1, 3)) + jp[r, 0, k] * inv[sym(0, l)]
    reduced = {}
    for a in range(8):
        for b in range(a, 8):
            k, r, m, s = a // 2, a % 2, b // 2, b % 2
            value = weighted[r, k, 0] * jp[s, 0, m] + weighted[r, k, 1] * jp[s, 1, m] + weighted[r, k, 2] * jp[s, 2, m]
            reduced[a, b] = 1.0 - value if a == b else -value

    def red(k, r, m, s):
        return reduced[sym(2 * k + r, 2 * m + s)]

    def camera(r, i, k):
        return load((9 * r + i) * 4 + k)

    for m in range(4):
        right = {(s, j): camera(s, j, m) for s in range(2) for j in range(9)}
        for j in range(9):
            parts = [
                rounded(right[0, j] * red(m, 0, m, s) + right[1, j] * red(m, 1, m, s)) * right[s, j]
                for s in range(2)
            ]
            dg_ref[pl.ds(m * 128 + j, 8, stride=16), :] = parts[0] + parts[1]
        for k in range(4):
            for which, i in enumerate((i_low, i_high)):
                left = [camera(r, i, k) for r in range(2)]
                mixed = [
                    rounded(left[0] * red(k, 0, m, s) + left[1] * red(k, 1, m, s)) for s in range(2)
                ]
                base = (which * 16 + k * 4 + m)
                for j in range(9):
                    value = mixed[0] * right[0, j] + mixed[1] * right[1, j]
                    if j < 8:
                        b_ref[pl.ds(base * 64 + j, 8, stride=8), :] = value
                    else:
                        b8_ref[pl.ds(base * 8, 8), :] = value


def twice(value):
    return jnp.concatenate([value, value], axis=0).astype(BF16)


def spread_row(ref, index):
    return jnp.broadcast_to(ref[pl.ds(index, 1), :], (8, 128))


def push_places(s, register, slot_ref, iota_ref):
    slots = [twice(spread_row(slot_ref, k * 8 + s)) for k in range(4)]
    zero = jnp.zeros((16, 128), BF16)
    one = jnp.ones((16, 128), BF16)
    places = [iota_ref[pl.ds(b * 16, 16), :] for b in range(16)]
    for unit in range(2):
        columns = [
            jnp.concatenate([jnp.where(slots[m] == value, one, zero) for value in places], axis=0)
            for m in (2 * unit, 2 * unit + 1)
        ]
        pltpu.matmul_push_rhs(jnp.concatenate(columns, axis=1), register, unit, transpose=True)
    return slots


def build_source(s, register, slots, accs, pb_ref, b_ref, b8_ref, dg_ref, target_ref, target8_ref, which_i):
    row = spread_row
    zero = jnp.zeros((16, 128), BF16)
    for which in range(2):
        for km in range(16):
            base = pl.multiple_of(((which * 16 + km) * 8 + s) * 8, 8)
            pb_ref[which, pl.ds(km * 16, 16), :] = twice(b_ref[pl.ds(base, 8), :])

    def choose(masks, values):
        value = zero
        for k in range(4):
            value = jnp.where(masks[k], values[k], value)
        return value

    def feed(block, parts):
        for unit in range(2):
            left = jnp.concatenate([parts[2 * unit], parts[2 * unit + 1]], axis=1)
            pltpu.matmul_acc_lhs(accs[unit][block], left, load_staged_rhs=register if block == 41 else None)

    parts = []
    for m in range(4):
        base = pl.multiple_of((m * 8 + s) * 16, 16)
        parts.append(dg_ref[pl.ds(base, 16), :].astype(BF16))
    feed(41, parts)
    for g in range(9):
        which = which_i[g]
        ops = [pb_ref[which, pl.ds(km * 16, 16), :] for km in range(16)]
        for b in range(4):
            target = target_ref[pl.ds((g * 4 + b) * 16, 16), :]
            masks = [slots[k] == target for k in range(4)]
            feed(g * 4 + b, [choose(masks, [ops[k * 4 + m] for k in range(4)]) for m in range(4)])
    for b in range(5):
        target = target8_ref[pl.ds(b * 16, 16), :]
        masks = [slots[k] == target for k in range(4)]
        low, high = which_i[2 * b], which_i[min(2 * b + 1, 8)]
        parts = []
        for m in range(4):
            values = []
            for k in range(4):
                km = k * 4 + m
                both = jnp.concatenate(
                    [row(b8_ref, (low * 16 + km) * 8 + s), row(b8_ref, (high * 16 + km) * 8 + s)], axis=0
                )
                values.append(both.astype(BF16))
            parts.append(choose(masks, values))
        feed(36 + b, parts)


def place(position):
    first_row = position * 72
    half = position // 16
    inside = first_row - half * 1152
    i_low = inside // 128
    start = inside - i_low * 128
    i_high = jnp.minimum(i_low + 1, 8)
    which_i = [(start + 8 * g) // 128 for g in range(9)]
    return half, start, i_low, i_high, which_i


def prepare(position, scr):
    dg_ref, target_ref, target8_ref, iota_ref = scr[3], scr[6], scr[7], scr[8]
    half, start, _, _, _ = place(position)

    def slot_of(r):
        return half * 128 + (start + r) % 128

    target_ref[...] = slot_of(iota((576, 128), 0) // 8).astype(F32).astype(BF16)
    row8 = iota((80, 128), 0)
    target8_ref[...] = jnp.where(row8 < 72, slot_of(row8), -2).astype(F32).astype(BF16)
    iota_ref[...] = iota((256, 128), 0).astype(F32).astype(BF16)
    dg_ref[...] = jnp.zeros_like(dg_ref)


def make_group(read_chunk, count, damp, position, dq_ref, scr, accs):
    (x_ref, b_ref, b8_ref, dg_ref, slot_ref, pb_ref, target_ref, target8_ref, iota_ref) = scr
    accs = (accs[:42], accs[42:])
    _, _, i_low, i_high, which_i = place(position)

    def group(row):
        def widen(s, carry):
            x_ref[pl.ds(pl.multiple_of(s * XROWS, 8), XROWS), :] = read_chunk(row * 8 + s)[:XROWS].astype(F32)
            return carry

        lax.fori_loop(0, 8, widen, 0)
        sub = iota((8, 128), 0)
        index = ((row * 4 + sub % 4) * 2 + sub // 4) * 128 + iota((8, 128), 1)
        point_blocks(x_ref, b_ref, b8_ref, dg_ref, slot_ref, damp, index < count, i_low, i_high)

        def sources(t, carry):
            first = t * UNROLL
            slots = {}
            for u in range(min(2, UNROLL)):
                slots[u] = push_places(first + u, u % 2, slot_ref, iota_ref)
            for u in range(UNROLL):
                build_source(
                    first + u, u % 2, slots[u], accs, pb_ref.at[u], b_ref, b8_ref, dg_ref, target_ref, target8_ref, which_i
                )
                if u + 2 < UNROLL:
                    slots[u + 2] = push_places(first + u + 2, u % 2, slot_ref, iota_ref)
            return carry

        lax.fori_loop(0, 8 // UNROLL, sources, 0)
        value = pltpu.matmul_pop(accs[0][41]) + pltpu.matmul_pop(accs[1][41])
        for h in range(2):
            dq_ref[row, h] = value[:, h * 128 : h * 128 + 128]

    def finish(acc_ref):
        for block in range(41):
            value = pltpu.matmul_pop(accs[0][block]) + pltpu.matmul_pop(accs[1][block])
            for h in range(2):
                acc_ref[h, pl.ds(block * 16, 16), :] = value[:, h * 128 : h * 128 + 128]

    return group, finish


def scratch():
    return [
        pltpu.VMEM((8 * XROWS, 128), F32),
        pltpu.VMEM((2 * 16 * 64, 128), F32),
        pltpu.VMEM((2 * 16 * 8, 128), F32),
        pltpu.VMEM((4 * 8 * 16, 128), F32),
        pltpu.VMEM((4 * 8, 128), F32),
        pltpu.VMEM((UNROLL, 2, 256, 128), BF16),
        pltpu.VMEM((576, 128), BF16),
        pltpu.VMEM((80, 128), BF16),
        pltpu.VMEM((256, 128), BF16),
    ]


def accumulators():
    return [pltpu.ACC(unit)((16, 256), F32) for unit in range(2) for _ in range(42)]


def unpack_tile(acc_ref, tile_ref):
    for g in range(9):
        for h in range(2):
            for j in range(8):
                tile_ref[pl.ds(g * 8, 8), pl.ds(h * 1152 + j * 128, 128)] = acc_ref[h, pl.ds(g * 64 + j, 8, stride=8), :]
            tile_ref[pl.ds(g * 8, 8), pl.ds(h * 1152 + 1024, 128)] = acc_ref[h, pl.ds(576 + g * 8, 8), :]


def total_diag(dq_ref, h):
    total = dq_ref[0, h]
    for n in range(1, 4):
        total = total + dq_ref[n, h]
    return total


MESH = pl.DeviceIdType.MESH
PTS = 32
CAM = 8


def here():
    return lax.axis_index("pts"), lax.axis_index("cam")


def plane_peer(d):
    pts, cam = here()
    return (pts + d) % PTS, cam


def line_peer(d):
    pts, cam = here()
    return pts, (cam + d) % CAM


def greet(plane, line):
    barrier = pltpu.get_barrier_semaphore()
    if plane:
        def one(d, carry):
            pl.semaphore_signal(barrier, inc=1, device_id=plane_peer(d), device_id_type=MESH)
            return carry

        lax.fori_loop(1, PTS, one, 0)
    if line:
        for d in range(1, CAM):
            pl.semaphore_signal(barrier, inc=1, device_id=line_peer(d), device_id_type=MESH)


def greeted(plane, line):
    pl.semaphore_wait(pltpu.get_barrier_semaphore(), (PTS - 1 if plane else 0) + (CAM - 1 if line else 0))


class Exchange:
    def __init__(self, plane, blocks, sem):
        self.size = PTS if plane else CAM
        self.peer = plane_peer if plane else line_peer
        self.me = here()[0 if plane else 1]
        self.blocks, self.sem = blocks, sem

    def copy(self, d):
        own = self.blocks(self.me, 1)
        return pltpu.make_async_remote_copy(
            src_ref=own, dst_ref=own, send_sem=self.sem.at[0], recv_sem=self.sem.at[1],
            device_id=self.peer(d), device_id_type=MESH,
        )

    def all_others(self):
        others = self.blocks(0, self.size - 1)
        return pltpu.make_async_remote_copy(
            src_ref=others, dst_ref=others, send_sem=self.sem.at[0], recv_sem=self.sem.at[1],
            device_id=self.peer(1), device_id_type=MESH,
        )

    def send(self):
        def one(d, carry):
            self.copy(d).start()
            return carry

        lax.fori_loop(1, self.size, one, 0)

    def receive(self):
        self.all_others().wait_recv()

    def sent(self):
        self.all_others().wait_send()


def blocks_of(ref, rows):
    return lambda first, count: ref.at[pl.ds(first * rows if isinstance(first, int) else pl.multiple_of(first * rows, rows), count * rows), :]


def pos_place(position):
    first_row = position * 72
    half = position // 16
    inside = first_row % 1152
    return half, inside // 128, inside % 128


def spread(ref, index):
    return jnp.broadcast_to(ref[pl.ds(index, 1), :], (8, 128))


def total_of(values):
    total = values[0]
    for value in values[1:]:
        total = total + value
    return jnp.sum(jnp.sum(total, axis=0, keepdims=True), axis=1, keepdims=True)


def solve(tile_ref, diag_block, groups_ref, damp, rhs_ref, out_ref, zd_ref, v_ref, zq_ref, pq_ref, zs_ref, ps_ref, sems, meanwhile, settle):
    position, cam = here()
    half, start, i_low, i_high, which_i = place(position)
    group_of = [groups_ref[0, 0], groups_ref[0, 1]]
    sub = iota((8, 128), 0)
    lane = iota((8, 128), 1)
    subf = sub.astype(F32)
    for h in range(2):
        tagged = jnp.where(iota((16, 128), 0) == 9, group_of[h].astype(F32), diag_block(h))
        zd_ref[pl.ds(pl.multiple_of((cam * 2 + h) * 16, 16), 16), :] = tagged
    zd = Exchange(False, blocks_of(zd_ref, 32), sems[0])
    zd.send()
    meanwhile()
    zd.receive()
    member = {(t, h): spread(zd_ref, (t * 2 + h) * 16 + 9) == subf for t in range(CAM) for h in range(2)}
    residual = [rhs_ref[i] for i in range(9)]
    diagonal = []
    for i in range(9):
        total = jnp.full((8, 128), damp, F32)
        for t in range(CAM):
            for h in range(2):
                total = total + jnp.where(member[t, h], spread(zd_ref, (t * 2 + h) * 16 + i), 0.0)
        diagonal.append(total)
    precond = [residual[i] / diagonal[i] for i in range(9)]
    inner = total_of([residual[i] * precond[i] for i in range(9)])
    own_member = [spread(zd_ref, (t * 2 + half) * 16 + 9) == subf for t in range(CAM)]

    def image_row(vector):
        for i in range(9):
            v_ref[pl.ds(i * 8, 8), :] = vector[i]
        ops = [[spread(v_ref, j * 8 + group_of[h]) for j in range(9)] for h in range(2)]
        placed = jnp.zeros((8, 128), F32)
        for g in range(9):
            total = None
            for h in range(2):
                for j in range(9):
                    term = tile_ref[pl.ds(g * 8, 8), pl.ds((h * 9 + j) * 128, 128)] * ops[h][j]
                    total = term if total is None else total + term
            value = jnp.sum(total, axis=1, keepdims=True)
            placed = placed + jnp.where(lane == (start + 8 * g + sub) % 128, value, 0.0)
        return jnp.sum(placed, axis=0, keepdims=True)

    zq_ref[pl.ds(cam, 1), :] = image_row(precond)
    zq = Exchange(False, blocks_of(zq_ref, 1), sems[1])
    zq.send()
    zq.receive()
    total = jnp.zeros((8, 128), F32)
    for t in range(CAM):
        total = total + jnp.where(own_member[t], spread(zq_ref, t), 0.0)
    pq_ref[pl.ds(pl.multiple_of(position * 8, 8), 8), :] = total
    pq = Exchange(True, blocks_of(pq_ref, 8), sems[2])
    pq.send()
    pq.receive()
    image = [damp * precond[i] for i in range(9)]
    for p in range(PTS):
        _, low, first = pos_place(p)
        value = pq_ref[pl.ds(p * 8, 8), :]
        if first + 72 > 128:
            image[low] = image[low] + jnp.where(lane >= first, value, 0.0)
            image[low + 1] = image[low + 1] + jnp.where(lane >= first, 0.0, value)
        else:
            image[low] = image[low] + value
    alpha = inner / total_of([precond[i] * image[i] for i in range(9)])
    residual = [residual[i] - alpha * image[i] for i in range(9)]
    scaled = [residual[i] / diagonal[i] for i in range(9)]
    inner_next = total_of([residual[i] * scaled[i] for i in range(9)])
    beta = inner_next / inner
    direction = [scaled[i] + beta * precond[i] for i in range(9)]
    row = image_row(direction)
    own_group = jnp.where(half == 0, group_of[0], group_of[1])
    lane_row = iota((1, 128), 1)
    own = jnp.where(
        lane_row >= start, v_ref[pl.ds(i_low * 8 + own_group, 1), :], v_ref[pl.ds(i_high * 8 + own_group, 1), :]
    )
    zs_ref[pl.ds(cam, 1), :] = row * own
    zs = Exchange(False, blocks_of(zs_ref, 1), sems[3])
    zs.send()
    for exchange in (zd, zq, pq):
        exchange.sent()
    settle()
    zs.receive()
    ps_ref[pl.ds(position, 1), :] = jnp.sum(zs_ref[...], axis=0, keepdims=True)
    ps = Exchange(True, blocks_of(ps_ref, 1), sems[4])
    ps.send()
    ps.receive()
    curvature = damp * total_of([value * value for value in direction]) + total_of(
        [ps_ref[pl.ds(8 * n, 8), :] for n in range(4)]
    )
    second = inner_next / curvature
    for i in range(9):
        out_ref[i] = alpha * precond[i] + second * direction[i]
    zs.sent()
    ps.sent()


def solve_scratch():
    return [
        pltpu.VMEM((CAM * 32, 128), F32),
        pltpu.VMEM((72, 128), F32),
        pltpu.VMEM((CAM, 128), F32),
        pltpu.VMEM((PTS * 8, 128), F32),
        pltpu.VMEM((CAM, 128), F32),
        pltpu.VMEM((PTS, 128), F32),
    ]


def solve_sems():
    return [pltpu.SemaphoreType.DMA((2,)) for _ in range(5)]


def plane_offsets():
    return [(dy, dx) for dy in (0, 3, 2, 1) for dx in range(4) if (dy, dx) != (0, 0)]


def whole_kernel(count_in, damp_in, groups_in, camera_in, point_in, obs_in, rhs_in, tile_out, out_ref, gbuf, tile_ref, acc_ref, dq_ref, *scr):
    work, rest = scr[:9], scr[9:]
    vectors, rest = rest[:6], rest[6:]
    sems, rest = rest[:5], rest[5:]
    send_sem, recv_sem, share_send, share_recv, load_sem = rest[:5]
    count_ref, damp_ref, groups_ref, camera_ref, point_ref, obs_ref, rhs_ref = rest[5:]
    position, cam = here()
    y, x, c = position // 8, position // 2 % 4, position % 2
    inputs = (count_in, damp_in, groups_in, camera_in, point_in, obs_in, rhs_in)
    loads = [pltpu.make_async_copy(src, dst, load_sem.at[n]) for n, (src, dst) in enumerate(zip(inputs, rest[5:]))]
    for load in loads:
        load.start()
    greet(True, True)
    for load in loads:
        load.wait()
    cameras = obs_ref[...]
    slot = jnp.where(cameras // 128 == groups_ref[0, 1], 128, 0) + cameras % 128
    chunk = jnp.concatenate(
        [camera_ref[...].astype(F32), point_ref[...].astype(F32), slot.astype(F32), jnp.zeros((12, 128), F32)], axis=0
    )
    gbuf[(y * 2 + c) * 4 + x] = chunk.astype(BF16)
    prepare(position, work)
    greeted(True, True)

    def spread_copy(dy, dx):
        own = gbuf.at[(y * 2 + c) * 4 + x]
        other = ((y + dy) % 4 * 4 + (x + dx) % 4) * 2 + c
        return pltpu.make_async_remote_copy(
            src_ref=own, dst_ref=own, send_sem=send_sem.at[0], recv_sem=recv_sem.at[y],
            device_id=(other, cam), device_id_type=MESH,
        )

    def chunks(first, count):
        where = gbuf.at[pl.ds(first, count)]
        return lambda send, recv: pltpu.make_async_remote_copy(
            src_ref=where, dst_ref=where, send_sem=send, recv_sem=recv,
            device_id=(position + 1 - 2 * c, cam), device_id_type=MESH,
        )

    def share(row, core):
        return chunks((row * 2 + core) * 4, 4)(share_send.at[row], share_recv.at[row])

    for dy, dx in plane_offsets():
        spread_copy(dy, dx).start()

    def hand_on(row, count):
        chunks((row * 2 + c) * 4, count)(send_sem.at[0], recv_sem.at[row]).wait_recv()
        share(row, c).start()

    def assemble(*accs):
        group, finish = make_group(lambda s: gbuf[s], count_ref[0, 0], damp_ref[0, 0], position, dq_ref, work, accs)
        hand_on(y, 3)
        hand_on((y + 1) % 4, 4)

        def one(step, carry):
            row = (y + step) % 4
            share(row, 1 - c).wait_recv()
            group(row)

            @pl.when(step < 2)
            def _():
                hand_on((y + step + 2) % 4, 4)

            return carry

        lax.fori_loop(0, 4, one, 0)
        finish(acc_ref)

    pl.run_scoped(assemble, *accumulators())
    store = pltpu.make_async_copy(tile_ref, tile_out, load_sem.at[7])

    def unpack():
        unpack_tile(acc_ref, tile_ref)
        store.start()

    def settle():
        store.wait()
        chunks(0, 15)(send_sem.at[0], recv_sem.at[0]).wait_send()
        for row in range(4):
            share(row, c).wait_send()

    solve(
        tile_ref, lambda h: total_diag(dq_ref, h), groups_ref, damp_ref[0, 0], rhs_ref, out_ref, *vectors, sems,
        unpack, settle,
    )


def hand_over(tile_in, solved_in, tile_out, solved_out, tile_buf, solved_buf, sem):
    pieces = [pl.ds(24 * n, 24) for n in range(3)]
    stages = [(tile_in.at[p, :], tile_buf.at[p, :], tile_out.at[p, :]) for p in pieces] + [(solved_in, solved_buf, solved_out)]
    loads = [pltpu.make_async_copy(src, buf, sem.at[0, n]) for n, (src, buf, _) in enumerate(stages)]
    stores = [pltpu.make_async_copy(buf, dst, sem.at[1, n]) for n, (_, buf, dst) in enumerate(stages)]
    for load in loads:
        load.start()
    for load, store in zip(loads, stores):
        load.wait()
        store.start()
    for store in stores:
        store.wait()


def body(jac_camera, jac_point, obs_camera, pair_groups, pair_points, damping, rhs):
    vm = pl.BlockSpec(memory_space=pltpu.VMEM)
    far = pl.BlockSpec(memory_space=pltpu.HBM)
    tile, solved = pl.pallas_call(
        whole_kernel,
        out_shape=(jax.ShapeDtypeStruct((72, 2304), F32), jax.ShapeDtypeStruct((9, 8, 128), F32)),
        in_specs=[far] * 7,
        out_specs=(far, vm),
        scratch_shapes=[pltpu.VMEM((PTS, ROWS, 128), BF16), pltpu.VMEM((72, 2304), F32), pltpu.VMEM((2, 656, 128), F32), pltpu.VMEM((4, 2, 16, 128), F32)]
        + scratch()
        + solve_scratch()
        + solve_sems()
        + [pltpu.SemaphoreType.DMA((n,)) for n in (1, 4, 4, 4, 8)]
        + [pltpu.SMEM((1, 1), jnp.int32), pltpu.SMEM((1, 1), F32), pltpu.SMEM((1, 2), jnp.int32)]
        + [pltpu.VMEM((72, 128), BF16), pltpu.VMEM((24, 128), BF16), pltpu.VMEM((4, 128), jnp.int32), pltpu.VMEM((9, 8, 128), F32)],
        compiler_params=pltpu.CompilerParams(collective_id=0, has_side_effects=True, vmem_limit_bytes=60 * 2**20),
        name="reduced_system",
    )(
        pair_points.reshape(1, 1), damping.reshape(1, 1), pair_groups, jac_camera[0].reshape(72, 128), jac_point[0].reshape(24, 128), obs_camera[0],
        rhs.transpose(1, 0, 2),
    )
    tile, solved = pl.pallas_call(
        hand_over,
        out_shape=(jax.ShapeDtypeStruct((72, 2304), F32), jax.ShapeDtypeStruct((9, 8, 128), F32)),
        in_specs=[far] * 2,
        out_specs=(far, far),
        scratch_shapes=[pltpu.VMEM((72, 2304), F32), pltpu.VMEM((9, 8, 128), F32), pltpu.SemaphoreType.DMA((2, 4))],
        compiler_params=pltpu.CompilerParams(vmem_limit_bytes=60 * 2**20),
        name="hand_over",
    )(tile, solved)
    return tile[None], solved.transpose(1, 0, 2)


def solution(mesh):
    placed = (P("cam", None, None, "pts"), P("cam", None, None, "pts"), P("cam", None, "pts"), P("cam", None), P("cam"), P(), P())
    return jax.shard_map(body, mesh=mesh, in_specs=placed, out_specs=(P("cam", "pts", None), P()), check_vma=False)
```

```python
import functools
import jax
import jax.numpy as jnp
from jax import lax
from jax.experimental import pallas as pl
from jax.experimental.pallas import tpu as pltpu
from jax.sharding import PartitionSpec as P

F32 = jnp.float32
BF16 = jnp.bfloat16
ROWS = 112
XROWS = 104
UNROLL = 4


def iota(shape, dim):
    return lax.broadcasted_iota(jnp.int32, shape, dim)


def sym(a, b):
    return (a, b) if a <= b else (b, a)


def rounded(value):
    return value.astype(BF16).astype(F32)


def geometry(load, damp):
    jp = {(r, j, k): load(72 + (3 * r + j) * 4 + k) for r in range(2) for j in range(3) for k in range(4)}
    normal = {}
    for a in range(3):
        for b in range(a, 3):
            total = None
            for k in range(4):
                for r in range(2):
                    term = jp[r, a, k] * jp[r, b, k]
                    total = term if total is None else total + term
            normal[a, b] = total + damp if a == b else total
    n00, n01, n02 = normal[0, 0], normal[0, 1], normal[0, 2]
    n11, n12, n22 = normal[1, 1], normal[1, 2], normal[2, 2]
    c00 = n11 * n22 - n12 * n12
    c01 = n02 * n12 - n01 * n22
    c02 = n01 * n12 - n02 * n11
    c11 = n00 * n22 - n02 * n02
    c12 = n01 * n02 - n00 * n12
    c22 = n00 * n11 - n01 * n01
    scale = 1.0 / (n00 * c00 + n01 * c01 + n02 * c02)
    inv = {(0, 0): c00 * scale, (0, 1): c01 * scale, (0, 2): c02 * scale,
           (1, 1): c11 * scale, (1, 2): c12 * scale, (2, 2): c22 * scale}
    weighted = {}
    for k in range(4):
        for r in range(2):
            for l in range(3):
                weighted[r, k, l] = sum(jp[r, j, k] * inv[sym(j, l)] for j in range(1, 3)) + jp[r, 0, k] * inv[sym(0, l)]
    reduced = {}
    for a in range(8):
        for b in range(a, 8):
            k, r, m, s = a // 2, a % 2, b // 2, b % 2
            value = weighted[r, k, 0] * jp[s, 0, m] + weighted[r, k, 1] * jp[s, 1, m] + weighted[r, k, 2] * jp[s, 2, m]
            reduced[a, b] = 1.0 - value if a == b else -value

    def red(k, r, m, s):
        return reduced[sym(2 * k + r, 2 * m + s)]

    return red


def own_diagonal(x_ref, dg_ref, damp):
    def load(q):
        return x_ref[pl.ds(q, 1), :]

    red = geometry(load, damp)
    for m in range(4):
        for j in range(9):
            jac = [load((9 * r + j) * 4 + m) for r in range(2)]
            parts = [rounded(jac[0] * red(m, 0, m, s) + jac[1] * red(m, 1, m, s)) * jac[s] for s in range(2)]
            dg_ref[pl.ds(m * 16 + j, 1), :] = parts[0] + parts[1]


def point_blocks(x_ref, b_ref, b8_ref, slot_ref, damp, live, i_low, i_high):
    def load(q):
        return x_ref[pl.ds(q, 8, stride=XROWS), :]

    for k in range(4):
        slot_ref[pl.ds(k * 8, 8), :] = jnp.where(live, load(96 + k), -1.0)
    red = geometry(load, damp)

    def camera(r, i, k):
        return load((9 * r + i) * 4 + k)

    for m in range(4):
        right = {(s, j): camera(s, j, m) for s in range(2) for j in range(9)}
        for k in range(4):
            for which, i in enumerate((i_low, i_high)):
                left = [camera(r, i, k) for r in range(2)]
                mixed = [
                    rounded(left[0] * red(k, 0, m, s) + left[1] * red(k, 1, m, s)) for s in range(2)
                ]
                base = (which * 16 + k * 4 + m)
                for j in range(9):
                    value = mixed[0] * right[0, j] + mixed[1] * right[1, j]
                    if j < 8:
                        b_ref[pl.ds(base * 64 + j, 8, stride=8), :] = value
                    else:
                        b8_ref[pl.ds(base * 8, 8), :] = value


def twice(value):
    return jnp.concatenate([value, value], axis=0).astype(BF16)


def spread_row(ref, index):
    return jnp.broadcast_to(ref[pl.ds(index, 1), :], (8, 128))


def push_places(s, register, slot_ref, iota_ref):
    slots = [twice(spread_row(slot_ref, k * 8 + s)) for k in range(4)]
    zero = jnp.zeros((16, 128), BF16)
    one = jnp.ones((16, 128), BF16)
    places = [iota_ref[pl.ds(b * 16, 16), :] for b in range(16)]
    for unit in range(2):
        columns = [
            jnp.concatenate([jnp.where(slots[m] == value, one, zero) for value in places], axis=0)
            for m in (2 * unit, 2 * unit + 1)
        ]
        pltpu.matmul_push_rhs(jnp.concatenate(columns, axis=1), register, unit, transpose=True)
    return slots


def build_source(s, register, slots, accs, pb_ref, b_ref, b8_ref, target_ref, target8_ref, which_i):
    row = spread_row
    zero = jnp.zeros((16, 128), BF16)
    for which in range(2):
        for km in range(16):
            base = pl.multiple_of(((which * 16 + km) * 8 + s) * 8, 8)
            pb_ref[which, pl.ds(km * 16, 16), :] = twice(b_ref[pl.ds(base, 8), :])

    def choose(masks, values):
        value = zero
        for k in range(4):
            value = jnp.where(masks[k], values[k], value)
        return value

    def feed(block, parts):
        for unit in range(2):
            left = jnp.concatenate([parts[2 * unit], parts[2 * unit + 1]], axis=1)
            pltpu.matmul_acc_lhs(accs[unit][block], left, load_staged_rhs=register if block == 0 else None)

    for g in range(9):
        which = which_i[g]
        ops = [pb_ref[which, pl.ds(km * 16, 16), :] for km in range(16)]
        for b in range(4):
            target = target_ref[pl.ds((g * 4 + b) * 16, 16), :]
            masks = [slots[k] == target for k in range(4)]
            feed(g * 4 + b, [choose(masks, [ops[k * 4 + m] for k in range(4)]) for m in range(4)])
    for b in range(5):
        target = target8_ref[pl.ds(b * 16, 16), :]
        masks = [slots[k] == target for k in range(4)]
        low, high = which_i[2 * b], which_i[min(2 * b + 1, 8)]
        parts = []
        for m in range(4):
            values = []
            for k in range(4):
                km = k * 4 + m
                both = jnp.concatenate(
                    [row(b8_ref, (low * 16 + km) * 8 + s), row(b8_ref, (high * 16 + km) * 8 + s)], axis=0
                )
                values.append(both.astype(BF16))
            parts.append(choose(masks, values))
        feed(36 + b, parts)


def place(position):
    first_row = position * 72
    half = position // 16
    inside = first_row - half * 1152
    i_low = inside // 128
    start = inside - i_low * 128
    i_high = jnp.minimum(i_low + 1, 8)
    which_i = [(start + 8 * g) // 128 for g in range(9)]
    return half, start, i_low, i_high, which_i


def prepare(position, scr):
    dg_ref, target_ref, target8_ref, iota_ref = scr[3], scr[6], scr[7], scr[8]
    half, start, _, _, _ = place(position)

    def slot_of(r):
        return half * 128 + (start + r) % 128

    target_ref[...] = slot_of(iota((576, 128), 0) // 8).astype(F32).astype(BF16)
    row8 = iota((80, 128), 0)
    target8_ref[...] = jnp.where(row8 < 72, slot_of(row8), -2).astype(F32).astype(BF16)
    iota_ref[...] = iota((256, 128), 0).astype(F32).astype(BF16)
    dg_ref[...] = jnp.zeros_like(dg_ref)


def make_group(read_chunk, count, damp, position, scr, accs):
    (x_ref, b_ref, b8_ref, _, slot_ref, pb_ref, target_ref, target8_ref, iota_ref) = scr
    accs = (accs[:41], accs[41:])
    _, _, i_low, i_high, which_i = place(position)

    def group(row):
        def widen(s, carry):
            x_ref[pl.ds(pl.multiple_of(s * XROWS, 8), XROWS), :] = read_chunk(row * 8 + s)[:XROWS].astype(F32)
            return carry

        lax.fori_loop(0, 8, widen, 0)
        sub = iota((8, 128), 0)
        index = ((row * 4 + sub % 4) * 2 + sub // 4) * 128 + iota((8, 128), 1)
        point_blocks(x_ref, b_ref, b8_ref, slot_ref, damp, index < count, i_low, i_high)

        def sources(t, carry):
            first = t * UNROLL
            slots = {}
            for u in range(min(2, UNROLL)):
                slots[u] = push_places(first + u, u % 2, slot_ref, iota_ref)
            for u in range(UNROLL):
                build_source(
                    first + u, u % 2, slots[u], accs, pb_ref.at[u], b_ref, b8_ref, target_ref, target8_ref, which_i
                )
                if u + 2 < UNROLL:
                    slots[u + 2] = push_places(first + u + 2, u % 2, slot_ref, iota_ref)
            return carry

        lax.fori_loop(0, 8 // UNROLL, sources, 0)

    def finish(acc_ref):
        for block in range(41):
            value = pltpu.matmul_pop(accs[0][block]) + pltpu.matmul_pop(accs[1][block])
            for h in range(2):
                acc_ref[h, pl.ds(block * 16, 16), :] = value[:, h * 128 : h * 128 + 128]

    return group, finish


def scratch():
    return [
        pltpu.VMEM((8 * XROWS, 128), F32),
        pltpu.VMEM((2 * 16 * 64, 128), F32),
        pltpu.VMEM((2 * 16 * 8, 128), F32),
        pltpu.VMEM((64, 128), F32),
        pltpu.VMEM((4 * 8, 128), F32),
        pltpu.VMEM((UNROLL, 2, 256, 128), BF16),
        pltpu.VMEM((576, 128), BF16),
        pltpu.VMEM((80, 128), BF16),
        pltpu.VMEM((256, 128), BF16),
    ]


def accumulators():
    return [pltpu.ACC(unit)((16, 256), F32) for unit in range(2) for _ in range(41)]


def unpack_tile(acc_ref, tile_ref):
    for g in range(9):
        for h in range(2):
            for j in range(8):
                tile_ref[pl.ds(g * 8, 8), pl.ds(h * 1152 + j * 128, 128)] = acc_ref[h, pl.ds(g * 64 + j, 8, stride=8), :]
            tile_ref[pl.ds(g * 8, 8), pl.ds(h * 1152 + 1024, 128)] = acc_ref[h, pl.ds(576 + g * 8, 8), :]


MESH = pl.DeviceIdType.MESH
PTS = 32
CAM = 8


def here():
    return lax.axis_index("pts"), lax.axis_index("cam")


def plane_peer(d):
    pts, cam = here()
    return (pts + d) % PTS, cam


def line_peer(d):
    pts, cam = here()
    return pts, (cam + d) % CAM


def greet(plane, line):
    barrier = pltpu.get_barrier_semaphore()
    if plane:
        def one(d, carry):
            pl.semaphore_signal(barrier, inc=1, device_id=plane_peer(d), device_id_type=MESH)
            return carry

        lax.fori_loop(1, PTS, one, 0)
    if line:
        for d in range(1, CAM):
            pl.semaphore_signal(barrier, inc=1, device_id=line_peer(d), device_id_type=MESH)


def greeted(plane, line):
    pl.semaphore_wait(pltpu.get_barrier_semaphore(), (PTS - 1 if plane else 0) + (CAM - 1 if line else 0))


class Exchange:
    def __init__(self, plane, blocks, sem):
        self.size = PTS if plane else CAM
        self.peer = plane_peer if plane else line_peer
        self.me = here()[0 if plane else 1]
        self.blocks, self.sem = blocks, sem

    def copy(self, d):
        own = self.blocks(self.me, 1)
        return pltpu.make_async_remote_copy(
            src_ref=own, dst_ref=own, send_sem=self.sem.at[0], recv_sem=self.sem.at[1],
            device_id=self.peer(d), device_id_type=MESH,
        )

    def all_others(self):
        others = self.blocks(0, self.size - 1)
        return pltpu.make_async_remote_copy(
            src_ref=others, dst_ref=others, send_sem=self.sem.at[0], recv_sem=self.sem.at[1],
            device_id=self.peer(1), device_id_type=MESH,
        )

    def send(self):
        def one(d, carry):
            self.copy(d).start()
            return carry

        lax.fori_loop(1, self.size, one, 0)

    def receive(self):
        self.all_others().wait_recv()

    def sent(self):
        self.all_others().wait_send()


def blocks_of(ref, rows):
    return lambda first, count: ref.at[pl.ds(first * rows if isinstance(first, int) else pl.multiple_of(first * rows, rows), count * rows), :]


def pos_place(position):
    first_row = position * 72
    half = position // 16
    inside = first_row % 1152
    return half, inside // 128, inside % 128


def spread(ref, index):
    return jnp.broadcast_to(ref[pl.ds(index, 1), :], (8, 128))


def total_of(values):
    total = values[0]
    for value in values[1:]:
        total = total + value
    return jnp.sum(jnp.sum(total, axis=0, keepdims=True), axis=1, keepdims=True)


def by_group(zd_ref, half, value):
    groups = iota((8, 128), 0).astype(F32)
    total = jnp.zeros((8, 128), F32)
    for t in range(CAM):
        total = total + jnp.where(spread(zd_ref, t * 8 + 1 + half) == groups, value(t), 0.0)
    return total


def solve(tile_ref, groups_ref, damp, rhs_ref, out_ref, zd_ref, pd_ref, v_ref, zq_ref, pq_ref, zs_ref, ps_ref, pd, sems, meanwhile, settle):
    position, cam = here()
    half, start, i_low, i_high, which_i = place(position)
    group_of = [groups_ref[0, 0], groups_ref[0, 1]]
    sub = iota((8, 128), 0)
    lane = iota((8, 128), 1)
    meanwhile()
    pd.receive()

    def assemble(ref, base):
        sums = list(base)
        for p in range(PTS):
            _, low, first = pos_place(p)
            value = ref[pl.ds(p * 8, 8), :]
            if first + 72 > 128:
                sums[low] = sums[low] + jnp.where(lane >= first, value, 0.0)
                sums[low + 1] = sums[low + 1] + jnp.where(lane >= first, 0.0, value)
            else:
                sums[low] = sums[low] + value
        return sums

    residual = [rhs_ref[i] for i in range(9)]
    diagonal = assemble(pd_ref, [jnp.full((8, 128), damp, F32)] * 9)
    precond = [residual[i] / diagonal[i] for i in range(9)]
    inner = total_of([residual[i] * precond[i] for i in range(9)])
    def image_row(vector):
        for i in range(9):
            v_ref[pl.ds(i * 8, 8), :] = vector[i]
        ops = [[spread(v_ref, j * 8 + group_of[h]) for j in range(9)] for h in range(2)]
        placed = jnp.zeros((8, 128), F32)
        for g in range(9):
            total = None
            for h in range(2):
                for j in range(9):
                    term = tile_ref[pl.ds(g * 8, 8), pl.ds((h * 9 + j) * 128, 128)] * ops[h][j]
                    total = term if total is None else total + term
            value = jnp.sum(total, axis=1, keepdims=True)
            placed = placed + jnp.where(lane == (start + 8 * g + sub) % 128, value, 0.0)
        return jnp.sum(placed, axis=0, keepdims=True)

    zq_ref[pl.ds(cam, 1), :] = image_row(precond)
    zq = Exchange(False, blocks_of(zq_ref, 1), sems[0])
    zq.send()
    zq.receive()
    total = by_group(zd_ref, half, lambda t: spread(zq_ref, t))
    pq_ref[pl.ds(pl.multiple_of(position * 8, 8), 8), :] = total
    pq = Exchange(True, blocks_of(pq_ref, 8), sems[1])
    pq.send()
    pq.receive()
    image = assemble(pq_ref, [damp * precond[i] for i in range(9)])
    alpha = inner / total_of([precond[i] * image[i] for i in range(9)])
    residual = [residual[i] - alpha * image[i] for i in range(9)]
    scaled = [residual[i] / diagonal[i] for i in range(9)]
    inner_next = total_of([residual[i] * scaled[i] for i in range(9)])
    beta = inner_next / inner
    direction = [scaled[i] + beta * precond[i] for i in range(9)]
    row = image_row(direction)
    own_group = jnp.where(half == 0, group_of[0], group_of[1])
    lane_row = iota((1, 128), 1)
    own = jnp.where(
        lane_row >= start, v_ref[pl.ds(i_low * 8 + own_group, 1), :], v_ref[pl.ds(i_high * 8 + own_group, 1), :]
    )
    zs_ref[pl.ds(cam, 1), :] = row * own
    zs = Exchange(False, blocks_of(zs_ref, 1), sems[2])
    zs.send()
    for exchange in (pd, zq, pq):
        exchange.sent()
    settle()
    zs.receive()
    ps_ref[pl.ds(position, 1), :] = jnp.sum(zs_ref[...], axis=0, keepdims=True)
    ps = Exchange(True, blocks_of(ps_ref, 1), sems[3])
    ps.send()
    ps.receive()
    curvature = damp * total_of([value * value for value in direction]) + total_of(
        [ps_ref[pl.ds(8 * n, 8), :] for n in range(4)]
    )
    second = inner_next / curvature
    for i in range(9):
        out_ref[i] = alpha * precond[i] + second * direction[i]
    zs.sent()
    ps.sent()


def solve_scratch():
    return [
        pltpu.VMEM((CAM * 8, 128), F32),
        pltpu.VMEM((PTS * 8, 128), F32),
        pltpu.VMEM((72, 128), F32),
        pltpu.VMEM((CAM, 128), F32),
        pltpu.VMEM((PTS * 8, 128), F32),
        pltpu.VMEM((CAM, 128), F32),
        pltpu.VMEM((PTS, 128), F32),
    ]


def solve_sems():
    return [pltpu.SemaphoreType.DMA((2,)) for _ in range(4)]


def plane_offsets():
    return [(dy, dx) for dy in (0, 3, 2, 1) for dx in range(4) if (dy, dx) != (0, 0)]


def partial_diagonal(x_ref, dg_ref, position, count, damp, part_ref, rows_out):
    own_diagonal(x_ref, dg_ref, damp)
    lane = iota((1, 128), 1)
    live = position * 128 + lane < count
    places = iota((256, 128), 0).astype(F32)
    left, right = [], []
    for k in range(4):
        slot = jnp.where(live, x_ref[pl.ds(96 + k, 1), :], -1.0)
        left.append(dg_ref[pl.ds(k * 16, 16), :].astype(BF16))
        right.append((jnp.broadcast_to(slot, (256, 128)) == places).astype(F32).astype(BF16))

    def product(*accs):
        for unit in range(2):
            pair = (2 * unit, 2 * unit + 1)
            pltpu.matmul_push_rhs(jnp.concatenate([right[k] for k in pair], axis=1), 0, unit, transpose=True)
            pltpu.matmul_acc_lhs(accs[unit], jnp.concatenate([left[k] for k in pair], axis=1), load_staged_rhs=0)
        value = pltpu.matmul_pop(accs[0]) + pltpu.matmul_pop(accs[1])
        for h in range(2):
            part_ref[h] = value[:, h * 128 : h * 128 + 128]

    pl.run_scoped(product, *[pltpu.ACC(unit)((16, 256), F32) for unit in range(2)])
    for p in range(PTS):
        h, low, first = pos_place(p)
        row = part_ref[h, low : low + 1, :]
        if first + 72 > 128:
            row = jnp.where(lane >= first, row, part_ref[h, low + 1 : low + 2, :])
        rows_out[p : p + 1, :] = row


def whole_kernel(count_in, damp_in, groups_in, camera_in, point_in, obs_in, rhs_in, tile_out, out_ref, gbuf, tile_ref, acc_ref, part_ref, rows_out, rows_in, *scr):
    work, rest = scr[:9], scr[9:]
    vectors, rest = rest[:7], rest[7:]
    sems, rest = rest[:4], rest[4:]
    send_sem, recv_sem, share_send, share_recv, load_sem, row_sem, zd_sem, pd_sem = rest[:8]
    count_ref, damp_ref, groups_ref, camera_ref, point_ref, obs_ref, rhs_ref = rest[8:]
    position, cam = here()
    y, x, c = position // 8, position // 2 % 4, position % 2
    inputs = (count_in, damp_in, groups_in, camera_in, point_in, obs_in, rhs_in)
    loads = [pltpu.make_async_copy(src, dst, load_sem.at[n]) for n, (src, dst) in enumerate(zip(inputs, rest[8:]))]
    for load in loads:
        load.start()
    greet(True, True)
    for load in loads:
        load.wait()
    cameras = obs_ref[...]
    slot = jnp.where(cameras // 128 == groups_ref[0, 1], 128, 0) + cameras % 128
    chunk = jnp.concatenate(
        [camera_ref[...].astype(F32), point_ref[...].astype(F32), slot.astype(F32), jnp.zeros((12, 128), F32)], axis=0
    )
    gbuf[(y * 2 + c) * 4 + x] = chunk.astype(BF16)
    prepare(position, work)
    damp = damp_ref[0, 0]
    half, start, _, _, _ = place(position)
    x_ref, dg_ref = work[0], work[3]
    x_ref[pl.ds(0, XROWS), :] = chunk[:XROWS]
    partial_diagonal(x_ref, dg_ref, position, count_ref[0, 0], damp, part_ref, rows_out)
    rows_in[pl.ds(position, 1), :] = rows_out[pl.ds(position, 1), :]
    greeted(True, True)

    def spread_copy(dy, dx):
        own = gbuf.at[(y * 2 + c) * 4 + x]
        other = ((y + dy) % 4 * 4 + (x + dx) % 4) * 2 + c
        return pltpu.make_async_remote_copy(
            src_ref=own, dst_ref=own, send_sem=send_sem.at[0], recv_sem=recv_sem.at[y],
            device_id=(other, cam), device_id_type=MESH,
        )

    def chunks(first, count):
        where = gbuf.at[pl.ds(first, count)]
        return lambda send, recv: pltpu.make_async_remote_copy(
            src_ref=where, dst_ref=where, send_sem=send, recv_sem=recv,
            device_id=(position + 1 - 2 * c, cam), device_id_type=MESH,
        )

    def share(row, core):
        return chunks((row * 2 + core) * 4, 4)(share_send.at[row], share_recv.at[row])

    for dy, dx in plane_offsets():
        spread_copy(dy, dx).start()

    def row_copy(d):
        other, _ = plane_peer(d)
        return pltpu.make_async_remote_copy(
            src_ref=rows_out.at[pl.ds(other, 1), :], dst_ref=rows_in.at[pl.ds(position, 1), :],
            send_sem=row_sem.at[0], recv_sem=row_sem.at[1], device_id=(other, cam), device_id_type=MESH,
        )

    def send_row(d, carry):
        row_copy(d).start()
        return carry

    lax.fori_loop(1, PTS, send_row, 0)

    def all_rows():
        return pltpu.make_async_remote_copy(
            src_ref=rows_out.at[pl.ds(0, PTS - 1), :], dst_ref=rows_in.at[pl.ds(0, PTS - 1), :],
            send_sem=row_sem.at[0], recv_sem=row_sem.at[1], device_id=plane_peer(1), device_id_type=MESH,
        )

    zd_ref, pd_ref = vectors[:2]
    zd = Exchange(False, blocks_of(zd_ref, 8), zd_sem)
    pd = Exchange(True, blocks_of(pd_ref, 8), pd_sem)

    def diagonal_rows():
        all_rows().wait_recv()
        own = jnp.sum(rows_in[...], axis=0, keepdims=True)
        sub = iota((8, 128), 0)
        mine = (iota((8, 128), 1) - start + 128) % 128 < 72
        first, second = groups_ref[0, 0].astype(F32), groups_ref[0, 1].astype(F32)
        value = jnp.where(sub == 0, jnp.where(mine, own, 0.0), jnp.where(sub == 1, first, second))
        zd_ref[pl.ds(pl.multiple_of(cam * 8, 8), 8), :] = value
        zd.send()

    def diagonal_groups():
        zd.receive()
        pd_ref[pl.ds(pl.multiple_of(position * 8, 8), 8), :] = by_group(zd_ref, half, lambda t: spread(zd_ref, t * 8))
        pd.send()

    def hand_on(row, count):
        chunks((row * 2 + c) * 4, count)(send_sem.at[0], recv_sem.at[row]).wait_recv()
        share(row, c).start()

    def assemble(*accs):
        group, finish = make_group(lambda s: gbuf[s], count_ref[0, 0], damp, position, work, accs)
        hand_on(y, 3)
        diagonal_rows()
        hand_on((y + 1) % 4, 4)

        def one(step, carry):
            row = (y + step) % 4
            share(row, 1 - c).wait_recv()
            group(row)

            @pl.when(step < 2)
            def _():
                hand_on((y + step + 2) % 4, 4)

            @pl.when(step == 1)
            def _():
                diagonal_groups()

            return carry

        lax.fori_loop(0, 4, one, 0)
        finish(acc_ref)

    pl.run_scoped(assemble, *accumulators())
    store = pltpu.make_async_copy(tile_ref, tile_out, load_sem.at[7])

    def unpack():
        unpack_tile(acc_ref, tile_ref)
        store.start()

    def settle():
        store.wait()
        all_rows().wait_send()
        zd.sent()
        chunks(0, 15)(send_sem.at[0], recv_sem.at[0]).wait_send()
        for row in range(4):
            share(row, c).wait_send()

    solve(
        tile_ref, groups_ref, damp, rhs_ref, out_ref, *vectors, pd, sems,
        unpack, settle,
    )


def hand_over(tile_in, solved_in, tile_out, solved_out, tile_buf, solved_buf, sem):
    pieces = [pl.ds(24 * n, 24) for n in range(3)]
    stages = [(tile_in.at[p, :], tile_buf.at[p, :], tile_out.at[p, :]) for p in pieces] + [(solved_in, solved_buf, solved_out)]
    loads = [pltpu.make_async_copy(src, buf, sem.at[0, n]) for n, (src, buf, _) in enumerate(stages)]
    stores = [pltpu.make_async_copy(buf, dst, sem.at[1, n]) for n, (_, buf, dst) in enumerate(stages)]
    for load in loads:
        load.start()
    for load, store in zip(loads, stores):
        load.wait()
        store.start()
    for store in stores:
        store.wait()


def body(jac_camera, jac_point, obs_camera, pair_groups, pair_points, damping, rhs):
    vm = pl.BlockSpec(memory_space=pltpu.VMEM)
    far = pl.BlockSpec(memory_space=pltpu.HBM)
    tile, solved = pl.pallas_call(
        whole_kernel,
        out_shape=(jax.ShapeDtypeStruct((72, 2304), F32), jax.ShapeDtypeStruct((9, 8, 128), F32)),
        in_specs=[far] * 7,
        out_specs=(far, vm),
        scratch_shapes=[pltpu.VMEM((PTS, ROWS, 128), BF16), pltpu.VMEM((72, 2304), F32), pltpu.VMEM((2, 656, 128), F32), pltpu.VMEM((2, 16, 128), F32)]
        + [pltpu.VMEM((PTS, 128), F32), pltpu.VMEM((PTS, 128), F32)]
        + scratch()
        + solve_scratch()
        + solve_sems()
        + [pltpu.SemaphoreType.DMA((n,)) for n in (1, 4, 4, 4, 8, 2, 2, 2)]
        + [pltpu.SMEM((1, 1), jnp.int32), pltpu.SMEM((1, 1), F32), pltpu.SMEM((1, 2), jnp.int32)]
        + [pltpu.VMEM((72, 128), BF16), pltpu.VMEM((24, 128), BF16), pltpu.VMEM((4, 128), jnp.int32), pltpu.VMEM((9, 8, 128), F32)],
        compiler_params=pltpu.CompilerParams(collective_id=0, has_side_effects=True, vmem_limit_bytes=60 * 2**20),
        name="reduced_system",
    )(
        pair_points.reshape(1, 1), damping.reshape(1, 1), pair_groups, jac_camera[0].reshape(72, 128), jac_point[0].reshape(24, 128), obs_camera[0],
        rhs.transpose(1, 0, 2),
    )
    tile, solved = pl.pallas_call(
        hand_over,
        out_shape=(jax.ShapeDtypeStruct((72, 2304), F32), jax.ShapeDtypeStruct((9, 8, 128), F32)),
        in_specs=[far] * 2,
        out_specs=(far, far),
        scratch_shapes=[pltpu.VMEM((72, 2304), F32), pltpu.VMEM((9, 8, 128), F32), pltpu.SemaphoreType.DMA((2, 4))],
        compiler_params=pltpu.CompilerParams(vmem_limit_bytes=60 * 2**20),
        name="hand_over",
    )(tile, solved)
    return tile[None], solved.transpose(1, 0, 2)


def solution(mesh):
    placed = (P("cam", None, None, "pts"), P("cam", None, None, "pts"), P("cam", None, "pts"), P("cam", None), P("cam"), P(), P())
    return jax.shard_map(body, mesh=mesh, in_specs=placed, out_specs=(P("cam", "pts", None), P()), check_vma=False)
```

```python
import functools
import jax
import jax.numpy as jnp
from jax import lax
from jax.experimental import pallas as pl
from jax.experimental.pallas import tpu as pltpu
from jax.sharding import PartitionSpec as P

F32 = jnp.float32
BF16 = jnp.bfloat16
ROWS = 112
XROWS = 104
UNROLL = 4


def iota(shape, dim):
    return lax.broadcasted_iota(jnp.int32, shape, dim)


def sym(a, b):
    return (a, b) if a <= b else (b, a)


def rounded(value):
    return value.astype(BF16).astype(F32)


def geometry(load, damp):
    jp = {(r, j, k): load(72 + (3 * r + j) * 4 + k) for r in range(2) for j in range(3) for k in range(4)}
    normal = {}
    for a in range(3):
        for b in range(a, 3):
            total = None
            for k in range(4):
                for r in range(2):
                    term = jp[r, a, k] * jp[r, b, k]
                    total = term if total is None else total + term
            normal[a, b] = total + damp if a == b else total
    n00, n01, n02 = normal[0, 0], normal[0, 1], normal[0, 2]
    n11, n12, n22 = normal[1, 1], normal[1, 2], normal[2, 2]
    c00 = n11 * n22 - n12 * n12
    c01 = n02 * n12 - n01 * n22
    c02 = n01 * n12 - n02 * n11
    c11 = n00 * n22 - n02 * n02
    c12 = n01 * n02 - n00 * n12
    c22 = n00 * n11 - n01 * n01
    scale = 1.0 / (n00 * c00 + n01 * c01 + n02 * c02)
    inv = {(0, 0): c00 * scale, (0, 1): c01 * scale, (0, 2): c02 * scale,
           (1, 1): c11 * scale, (1, 2): c12 * scale, (2, 2): c22 * scale}
    weighted = {}
    for k in range(4):
        for r in range(2):
            for l in range(3):
                weighted[r, k, l] = sum(jp[r, j, k] * inv[sym(j, l)] for j in range(1, 3)) + jp[r, 0, k] * inv[sym(0, l)]
    reduced = {}
    for a in range(8):
        for b in range(a, 8):
            k, r, m, s = a // 2, a % 2, b // 2, b % 2
            value = weighted[r, k, 0] * jp[s, 0, m] + weighted[r, k, 1] * jp[s, 1, m] + weighted[r, k, 2] * jp[s, 2, m]
            reduced[a, b] = 1.0 - value if a == b else -value

    def red(k, r, m, s):
        return reduced[sym(2 * k + r, 2 * m + s)]

    return red


def own_diagonal(x_ref, dg_ref, damp):
    def load(q):
        return x_ref[pl.ds(q, 1), :]

    red = geometry(load, damp)
    for m in range(4):
        for j in range(9):
            jac = [load((9 * r + j) * 4 + m) for r in range(2)]
            parts = [rounded(jac[0] * red(m, 0, m, s) + jac[1] * red(m, 1, m, s)) * jac[s] for s in range(2)]
            dg_ref[pl.ds(m * 16 + j, 1), :] = parts[0] + parts[1]


def point_blocks(x_ref, b_ref, b8_ref, slot_ref, damp, live, i_low, i_high):
    def load(q):
        return x_ref[pl.ds(q, 8, stride=XROWS), :]

    for k in range(4):
        slot_ref[pl.ds(k * 8, 8), :] = jnp.where(live, load(96 + k), -1.0)
    red = geometry(load, damp)

    def camera(r, i, k):
        return load((9 * r + i) * 4 + k)

    for m in range(4):
        right = {(s, j): camera(s, j, m) for s in range(2) for j in range(9)}
        for k in range(4):
            for which, i in enumerate((i_low, i_high)):
                left = [camera(r, i, k) for r in range(2)]
                mixed = [
                    rounded(left[0] * red(k, 0, m, s) + left[1] * red(k, 1, m, s)) for s in range(2)
                ]
                base = (which * 16 + k * 4 + m)
                for j in range(9):
                    value = mixed[0] * right[0, j] + mixed[1] * right[1, j]
                    if j < 8:
                        b_ref[pl.ds(base * 64 + j, 8, stride=8), :] = value
                    else:
                        b8_ref[pl.ds(base * 8, 8), :] = value


def twice(value):
    return jnp.concatenate([value, value], axis=0).astype(BF16)


def spread_row(ref, index):
    return jnp.broadcast_to(ref[pl.ds(index, 1), :], (8, 128))


def push_places(s, register, slot_ref, iota_ref):
    slots = [twice(spread_row(slot_ref, k * 8 + s)) for k in range(4)]
    zero = jnp.zeros((16, 128), BF16)
    one = jnp.ones((16, 128), BF16)
    places = [iota_ref[pl.ds(b * 16, 16), :] for b in range(16)]
    for unit in range(2):
        columns = [
            jnp.concatenate([jnp.where(slots[m] == value, one, zero) for value in places], axis=0)
            for m in (2 * unit, 2 * unit + 1)
        ]
        pltpu.matmul_push_rhs(jnp.concatenate(columns, axis=1), register, unit, transpose=True)
    return slots


def build_source(s, register, slots, accs, pb_ref, b_ref, b8_ref, target_ref, target8_ref, which_i):
    row = spread_row
    zero = jnp.zeros((16, 128), BF16)
    for which in range(2):
        for km in range(16):
            base = pl.multiple_of(((which * 16 + km) * 8 + s) * 8, 8)
            pb_ref[which, pl.ds(km * 16, 16), :] = twice(b_ref[pl.ds(base, 8), :])

    def choose(masks, values):
        value = zero
        for k in range(4):
            value = jnp.where(masks[k], values[k], value)
        return value

    def feed(block, parts):
        for unit in range(2):
            left = jnp.concatenate([parts[2 * unit], parts[2 * unit + 1]], axis=1)
            pltpu.matmul_acc_lhs(accs[unit][block], left, load_staged_rhs=register if block == 0 else None)

    for g in range(9):
        which = which_i[g]
        ops = [pb_ref[which, pl.ds(km * 16, 16), :] for km in range(16)]
        for b in range(4):
            target = target_ref[pl.ds((g * 4 + b) * 16, 16), :]
            masks = [slots[k] == target for k in range(4)]
            feed(g * 4 + b, [choose(masks, [ops[k * 4 + m] for k in range(4)]) for m in range(4)])
    for b in range(5):
        target = target8_ref[pl.ds(b * 16, 16), :]
        masks = [slots[k] == target for k in range(4)]
        low, high = which_i[2 * b], which_i[min(2 * b + 1, 8)]
        parts = []
        for m in range(4):
            values = []
            for k in range(4):
                km = k * 4 + m
                both = jnp.concatenate(
                    [row(b8_ref, (low * 16 + km) * 8 + s), row(b8_ref, (high * 16 + km) * 8 + s)], axis=0
                )
                values.append(both.astype(BF16))
            parts.append(choose(masks, values))
        feed(36 + b, parts)


def place(position):
    first_row = position * 72
    half = position // 16
    inside = first_row - half * 1152
    i_low = inside // 128
    start = inside - i_low * 128
    i_high = jnp.minimum(i_low + 1, 8)
    which_i = [(start + 8 * g) // 128 for g in range(9)]
    return half, start, i_low, i_high, which_i


def prepare(position, scr):
    dg_ref, target_ref, target8_ref, iota_ref = scr[3], scr[6], scr[7], scr[8]
    half, start, _, _, _ = place(position)

    def slot_of(r):
        return half * 128 + (start + r) % 128

    target_ref[...] = slot_of(iota((576, 128), 0) // 8).astype(F32).astype(BF16)
    row8 = iota((80, 128), 0)
    target8_ref[...] = jnp.where(row8 < 72, slot_of(row8), -2).astype(F32).astype(BF16)
    iota_ref[...] = iota((256, 128), 0).astype(F32).astype(BF16)
    dg_ref[...] = jnp.zeros_like(dg_ref)


def make_group(read_chunk, count, damp, position, scr, accs):
    (x_ref, b_ref, b8_ref, _, slot_ref, pb_ref, target_ref, target8_ref, iota_ref) = scr
    accs = (accs[:41], accs[41:])
    _, _, i_low, i_high, which_i = place(position)

    def group(row):
        def widen(s, carry):
            x_ref[pl.ds(pl.multiple_of(s * XROWS, 8), XROWS), :] = read_chunk(row * 8 + s)[:XROWS].astype(F32)
            return carry

        lax.fori_loop(0, 8, widen, 0)
        sub = iota((8, 128), 0)
        index = ((row * 4 + sub % 4) * 2 + sub // 4) * 128 + iota((8, 128), 1)
        point_blocks(x_ref, b_ref, b8_ref, slot_ref, damp, index < count, i_low, i_high)

        def sources(t, carry):
            first = t * UNROLL
            slots = {}
            for u in range(min(2, UNROLL)):
                slots[u] = push_places(first + u, u % 2, slot_ref, iota_ref)
            for u in range(UNROLL):
                build_source(
                    first + u, u % 2, slots[u], accs, pb_ref.at[u], b_ref, b8_ref, target_ref, target8_ref, which_i
                )
                if u + 2 < UNROLL:
                    slots[u + 2] = push_places(first + u + 2, u % 2, slot_ref, iota_ref)
            return carry

        lax.fori_loop(0, 8 // UNROLL, sources, 0)

    def finish(acc_ref):
        for block in range(41):
            value = pltpu.matmul_pop(accs[0][block]) + pltpu.matmul_pop(accs[1][block])
            for h in range(2):
                acc_ref[h, pl.ds(block * 16, 16), :] = value[:, h * 128 : h * 128 + 128]

    return group, finish


def scratch():
    return [
        pltpu.VMEM((8 * XROWS, 128), F32),
        pltpu.VMEM((2 * 16 * 64, 128), F32),
        pltpu.VMEM((2 * 16 * 8, 128), F32),
        pltpu.VMEM((64, 128), F32),
        pltpu.VMEM((4 * 8, 128), F32),
        pltpu.VMEM((UNROLL, 2, 256, 128), BF16),
        pltpu.VMEM((576, 128), BF16),
        pltpu.VMEM((80, 128), BF16),
        pltpu.VMEM((256, 128), BF16),
    ]


def accumulators():
    return [pltpu.ACC(unit)((16, 256), F32) for unit in range(2) for _ in range(41)]


def unpack_tile(acc_ref, tile_ref):
    for g in range(9):
        for h in range(2):
            for j in range(8):
                tile_ref[pl.ds(g * 8, 8), pl.ds(h * 1152 + j * 128, 128)] = acc_ref[h, pl.ds(g * 64 + j, 8, stride=8), :]
            tile_ref[pl.ds(g * 8, 8), pl.ds(h * 1152 + 1024, 128)] = acc_ref[h, pl.ds(576 + g * 8, 8), :]


MESH = pl.DeviceIdType.MESH
PTS = 32
CAM = 8


def here():
    return lax.axis_index("pts"), lax.axis_index("cam")


def plane_peer(d):
    pts, cam = here()
    return (pts + d) % PTS, cam


def line_peer(d):
    pts, cam = here()
    return pts, (cam + d) % CAM


def greet(plane, line):
    barrier = pltpu.get_barrier_semaphore()
    if plane:
        def one(d, carry):
            pl.semaphore_signal(barrier, inc=1, device_id=plane_peer(d), device_id_type=MESH)
            return carry

        lax.fori_loop(1, PTS, one, 0)
    if line:
        for d in range(1, CAM):
            pl.semaphore_signal(barrier, inc=1, device_id=line_peer(d), device_id_type=MESH)


def greeted(plane, line):
    pl.semaphore_wait(pltpu.get_barrier_semaphore(), (PTS - 1 if plane else 0) + (CAM - 1 if line else 0))


class Exchange:
    def __init__(self, plane, blocks, sem):
        self.size = PTS if plane else CAM
        self.peer = plane_peer if plane else line_peer
        self.me = here()[0 if plane else 1]
        self.blocks, self.sem = blocks, sem

    def copy(self, d):
        own = self.blocks(self.me, 1)
        return pltpu.make_async_remote_copy(
            src_ref=own, dst_ref=own, send_sem=self.sem.at[0], recv_sem=self.sem.at[1],
            device_id=self.peer(d), device_id_type=MESH,
        )

    def all_others(self):
        others = self.blocks(0, self.size - 1)
        return pltpu.make_async_remote_copy(
            src_ref=others, dst_ref=others, send_sem=self.sem.at[0], recv_sem=self.sem.at[1],
            device_id=self.peer(1), device_id_type=MESH,
        )

    def send(self):
        def one(d, carry):
            self.copy(d).start()
            return carry

        lax.fori_loop(1, self.size, one, 0)

    def receive(self):
        self.all_others().wait_recv()

    def sent(self):
        self.all_others().wait_send()


def blocks_of(ref, rows):
    return lambda first, count: ref.at[pl.ds(first * rows if isinstance(first, int) else pl.multiple_of(first * rows, rows), count * rows), :]


def pos_place(position):
    first_row = position * 72
    half = position // 16
    inside = first_row % 1152
    return half, inside // 128, inside % 128


def spread(ref, index):
    return jnp.broadcast_to(ref[pl.ds(index, 1), :], (8, 128))


def total_of(values):
    total = values[0]
    for value in values[1:]:
        total = total + value
    return jnp.sum(jnp.sum(total, axis=0, keepdims=True), axis=1, keepdims=True)


def by_group(zd_ref, half, value):
    groups = iota((8, 128), 0).astype(F32)
    total = jnp.zeros((8, 128), F32)
    for t in range(CAM):
        total = total + jnp.where(spread(zd_ref, t * 8 + 1 + half) == groups, value(t), 0.0)
    return total


def solve(tile_ref, groups_ref, damp, rhs_ref, out_ref, zd_ref, pd_ref, v_ref, zq_ref, pq_ref, zs_ref, ps_ref, pd, sems, meanwhile, settle):
    position, cam = here()
    half, start, i_low, i_high, which_i = place(position)
    group_of = [groups_ref[0, 0], groups_ref[0, 1]]
    sub = iota((8, 128), 0)
    lane = iota((8, 128), 1)
    meanwhile()
    pd.receive()

    def assemble(ref, base):
        sums = list(base)
        for p in range(PTS):
            _, low, first = pos_place(p)
            value = ref[pl.ds(p * 8, 8), :]
            if first + 72 > 128:
                sums[low] = sums[low] + jnp.where(lane >= first, value, 0.0)
                sums[low + 1] = sums[low + 1] + jnp.where(lane >= first, 0.0, value)
            else:
                sums[low] = sums[low] + value
        return sums

    residual = [rhs_ref[i] for i in range(9)]
    diagonal = assemble(pd_ref, [jnp.full((8, 128), damp, F32)] * 9)
    precond = [residual[i] / diagonal[i] for i in range(9)]
    inner = total_of([residual[i] * precond[i] for i in range(9)])
    def image_row(vector):
        for i in range(9):
            v_ref[pl.ds(i * 8, 8), :] = vector[i]
        ops = [[spread(v_ref, j * 8 + group_of[h]) for j in range(9)] for h in range(2)]
        placed = jnp.zeros((8, 128), F32)
        for g in range(9):
            total = None
            for h in range(2):
                for j in range(9):
                    term = tile_ref[pl.ds(g * 8, 8), pl.ds((h * 9 + j) * 128, 128)] * ops[h][j]
                    total = term if total is None else total + term
            value = jnp.sum(total, axis=1, keepdims=True)
            placed = placed + jnp.where(lane == (start + 8 * g + sub) % 128, value, 0.0)
        return jnp.sum(placed, axis=0, keepdims=True)

    zq_ref[pl.ds(cam, 1), :] = image_row(precond)
    zq = Exchange(False, blocks_of(zq_ref, 1), sems[0])
    zq.send()
    zq.receive()
    total = by_group(zd_ref, half, lambda t: spread(zq_ref, t))
    pq_ref[pl.ds(pl.multiple_of(position * 8, 8), 8), :] = total
    pq = Exchange(True, blocks_of(pq_ref, 8), sems[1])
    pq.send()
    pq.receive()
    image = assemble(pq_ref, [damp * precond[i] for i in range(9)])
    alpha = inner / total_of([precond[i] * image[i] for i in range(9)])
    residual = [residual[i] - alpha * image[i] for i in range(9)]
    scaled = [residual[i] / diagonal[i] for i in range(9)]
    inner_next = total_of([residual[i] * scaled[i] for i in range(9)])
    beta = inner_next / inner
    direction = [scaled[i] + beta * precond[i] for i in range(9)]
    row = image_row(direction)
    own_group = jnp.where(half == 0, group_of[0], group_of[1])
    lane_row = iota((1, 128), 1)
    own = jnp.where(
        lane_row >= start, v_ref[pl.ds(i_low * 8 + own_group, 1), :], v_ref[pl.ds(i_high * 8 + own_group, 1), :]
    )
    zs_ref[pl.ds(cam, 1), :] = row * own
    zs = Exchange(False, blocks_of(zs_ref, 1), sems[2])
    zs.send()
    for exchange in (pd, zq, pq):
        exchange.sent()
    settle()
    zs.receive()
    ps_ref[pl.ds(position, 1), :] = jnp.sum(zs_ref[...], axis=0, keepdims=True)
    ps = Exchange(True, blocks_of(ps_ref, 1), sems[3])
    ps.send()
    ps.receive()
    curvature = damp * total_of([value * value for value in direction]) + total_of(
        [ps_ref[pl.ds(8 * n, 8), :] for n in range(4)]
    )
    second = inner_next / curvature
    for i in range(9):
        out_ref[i] = alpha * precond[i] + second * direction[i]
    zs.sent()
    ps.sent()


def solve_scratch():
    return [
        pltpu.VMEM((CAM * 8, 128), F32),
        pltpu.VMEM((PTS * 8, 128), F32),
        pltpu.VMEM((72, 128), F32),
        pltpu.VMEM((CAM, 128), F32),
        pltpu.VMEM((PTS * 8, 128), F32),
        pltpu.VMEM((CAM, 128), F32),
        pltpu.VMEM((PTS, 128), F32),
    ]


def solve_sems():
    return [pltpu.SemaphoreType.DMA((2,)) for _ in range(4)]


def near_offsets():
    return [(0, dx, dc) for dc in range(2) for dx in range(4) if (dx, dc) != (0, 0)]


def far_offsets():
    return [(dy, dx, 0) for dy in (3, 2, 1) for dx in range(4)]


def partial_diagonal(x_ref, dg_ref, position, count, damp, part_ref, rows_out):
    own_diagonal(x_ref, dg_ref, damp)
    lane = iota((1, 128), 1)
    live = position * 128 + lane < count
    places = iota((256, 128), 0).astype(F32)
    left, right = [], []
    for k in range(4):
        slot = jnp.where(live, x_ref[pl.ds(96 + k, 1), :], -1.0)
        left.append(dg_ref[pl.ds(k * 16, 16), :].astype(BF16))
        right.append((jnp.broadcast_to(slot, (256, 128)) == places).astype(F32).astype(BF16))

    def product(*accs):
        for unit in range(2):
            pair = (2 * unit, 2 * unit + 1)
            pltpu.matmul_push_rhs(jnp.concatenate([right[k] for k in pair], axis=1), 0, unit, transpose=True)
            pltpu.matmul_acc_lhs(accs[unit], jnp.concatenate([left[k] for k in pair], axis=1), load_staged_rhs=0)
        value = pltpu.matmul_pop(accs[0]) + pltpu.matmul_pop(accs[1])
        for h in range(2):
            part_ref[h] = value[:, h * 128 : h * 128 + 128]

    pl.run_scoped(product, *[pltpu.ACC(unit)((16, 256), F32) for unit in range(2)])
    for p in range(PTS):
        h, low, first = pos_place(p)
        row = part_ref[h, low : low + 1, :]
        if first + 72 > 128:
            row = jnp.where(lane >= first, row, part_ref[h, low + 1 : low + 2, :])
        rows_out[p : p + 1, :] = row


def whole_kernel(count_in, damp_in, groups_in, camera_in, point_in, obs_in, rhs_in, tile_out, out_ref, gbuf, tile_ref, acc_ref, part_ref, rows_out, rows_in, *scr):
    work, rest = scr[:9], scr[9:]
    vectors, rest = rest[:7], rest[7:]
    sems, rest = rest[:4], rest[4:]
    send_sem, recv_sem, share_send, share_recv, load_sem, row_sem, zd_sem, pd_sem = rest[:8]
    count_ref, damp_ref, groups_ref, camera_ref, point_ref, obs_ref, rhs_ref = rest[8:]
    position, cam = here()
    y, x, c = position // 8, position // 2 % 4, position % 2
    inputs = (count_in, damp_in, groups_in, camera_in, point_in, obs_in, rhs_in)
    loads = [pltpu.make_async_copy(src, dst, load_sem.at[n]) for n, (src, dst) in enumerate(zip(inputs, rest[8:]))]
    for load in loads:
        load.start()
    greet(True, True)
    prepare(position, work)
    for load in loads:
        load.wait()
    cameras = obs_ref[...]
    slot = jnp.where(cameras // 128 == groups_ref[0, 1], 128, 0) + cameras % 128
    chunk = jnp.concatenate(
        [camera_ref[...].astype(F32), point_ref[...].astype(F32), slot.astype(F32), jnp.zeros((12, 128), F32)], axis=0
    )
    gbuf[(y * 2 + c) * 4 + x] = chunk.astype(BF16)
    damp = damp_ref[0, 0]
    half, start, _, _, _ = place(position)
    x_ref, dg_ref = work[0], work[3]
    x_ref[pl.ds(0, XROWS), :] = chunk[:XROWS]
    partial_diagonal(x_ref, dg_ref, position, count_ref[0, 0], damp, part_ref, rows_out)
    rows_in[pl.ds(position, 1), :] = rows_out[pl.ds(position, 1), :]
    greeted(True, True)

    def spread_copy(dy, dx, dc):
        own = gbuf.at[(y * 2 + c) * 4 + x]
        other = ((y + dy) % 4 * 4 + (x + dx) % 4) * 2 + (c + dc) % 2
        return pltpu.make_async_remote_copy(
            src_ref=own, dst_ref=own, send_sem=send_sem.at[0], recv_sem=recv_sem.at[y],
            device_id=(other, cam), device_id_type=MESH,
        )

    def chunks(first, count):
        where = gbuf.at[pl.ds(first, count)]
        return lambda send, recv: pltpu.make_async_remote_copy(
            src_ref=where, dst_ref=where, send_sem=send, recv_sem=recv,
            device_id=(position + 1 - 2 * c, cam), device_id_type=MESH,
        )

    def share(row, core):
        return chunks((row * 2 + core) * 4, 4)(share_send.at[row], share_recv.at[row])

    for offset in near_offsets():
        spread_copy(*offset).start()

    def row_copy(d):
        other, _ = plane_peer(d)
        return pltpu.make_async_remote_copy(
            src_ref=rows_out.at[pl.ds(other, 1), :], dst_ref=rows_in.at[pl.ds(position, 1), :],
            send_sem=row_sem.at[0], recv_sem=row_sem.at[1], device_id=(other, cam), device_id_type=MESH,
        )

    def send_row(d, carry):
        row_copy(d).start()
        return carry

    lax.fori_loop(1, PTS, send_row, 0)
    for offset in far_offsets():
        spread_copy(*offset).start()

    def all_rows():
        return pltpu.make_async_remote_copy(
            src_ref=rows_out.at[pl.ds(0, PTS - 1), :], dst_ref=rows_in.at[pl.ds(0, PTS - 1), :],
            send_sem=row_sem.at[0], recv_sem=row_sem.at[1], device_id=plane_peer(1), device_id_type=MESH,
        )

    zd_ref, pd_ref = vectors[:2]
    zd = Exchange(False, blocks_of(zd_ref, 8), zd_sem)
    pd = Exchange(True, blocks_of(pd_ref, 8), pd_sem)

    def diagonal_rows():
        all_rows().wait_recv()
        own = jnp.sum(rows_in[...], axis=0, keepdims=True)
        sub = iota((8, 128), 0)
        mine = (iota((8, 128), 1) - start + 128) % 128 < 72
        first, second = groups_ref[0, 0].astype(F32), groups_ref[0, 1].astype(F32)
        value = jnp.where(sub == 0, jnp.where(mine, own, 0.0), jnp.where(sub == 1, first, second))
        zd_ref[pl.ds(pl.multiple_of(cam * 8, 8), 8), :] = value
        zd.send()

    def diagonal_groups():
        zd.receive()
        pd_ref[pl.ds(pl.multiple_of(position * 8, 8), 8), :] = by_group(zd_ref, half, lambda t: spread(zd_ref, t * 8))
        pd.send()

    def hand_on(row):
        chunks((row * 2 + c) * 4, 4)(send_sem.at[0], recv_sem.at[row]).wait_recv()
        share(row, c).start()

    def assemble(*accs):
        group, finish = make_group(lambda s: gbuf[s], count_ref[0, 0], damp, position, work, accs)
        diagonal_rows()
        chunks(y * 8, 7)(send_sem.at[0], recv_sem.at[y]).wait_recv()
        hand_on((y + 1) % 4)

        def one(step, carry):
            row = (y + step) % 4

            @pl.when(step > 0)
            def _():
                share(row, 1 - c).wait_recv()

            group(row)

            @pl.when(step == 0)
            def _():
                hand_on((y + 2) % 4)

            @pl.when(step == 1)
            def _():
                hand_on((y + 3) % 4)
                diagonal_groups()

            return carry

        lax.fori_loop(0, 4, one, 0)
        finish(acc_ref)

    pl.run_scoped(assemble, *accumulators())
    store = pltpu.make_async_copy(tile_ref, tile_out, load_sem.at[7])

    def unpack():
        unpack_tile(acc_ref, tile_ref)
        store.start()

    def settle():
        store.wait()
        all_rows().wait_send()
        zd.sent()
        chunks(0, 19)(send_sem.at[0], recv_sem.at[0]).wait_send()
        for step in range(1, 4):
            share((y + step) % 4, c).wait_send()

    solve(
        tile_ref, groups_ref, damp, rhs_ref, out_ref, *vectors, pd, sems,
        unpack, settle,
    )


def hand_over(tile_in, solved_in, tile_out, solved_out, tile_buf, solved_buf, sem):
    pieces = [pl.ds(24 * n, 24) for n in range(3)]
    stages = [(tile_in.at[p, :], tile_buf.at[p, :], tile_out.at[p, :]) for p in pieces] + [(solved_in, solved_buf, solved_out)]
    loads = [pltpu.make_async_copy(src, buf, sem.at[0, n]) for n, (src, buf, _) in enumerate(stages)]
    stores = [pltpu.make_async_copy(buf, dst, sem.at[1, n]) for n, (_, buf, dst) in enumerate(stages)]
    for load in loads:
        load.start()
    for load, store in zip(loads, stores):
        load.wait()
        store.start()
    for store in stores:
        store.wait()


def body(jac_camera, jac_point, obs_camera, pair_groups, pair_points, damping, rhs):
    vm = pl.BlockSpec(memory_space=pltpu.VMEM)
    far = pl.BlockSpec(memory_space=pltpu.HBM)
    tile, solved = pl.pallas_call(
        whole_kernel,
        out_shape=(jax.ShapeDtypeStruct((72, 2304), F32), jax.ShapeDtypeStruct((9, 8, 128), F32)),
        in_specs=[far] * 7,
        out_specs=(far, vm),
        scratch_shapes=[pltpu.VMEM((PTS, ROWS, 128), BF16), pltpu.VMEM((72, 2304), F32), pltpu.VMEM((2, 656, 128), F32), pltpu.VMEM((2, 16, 128), F32)]
        + [pltpu.VMEM((PTS, 128), F32), pltpu.VMEM((PTS, 128), F32)]
        + scratch()
        + solve_scratch()
        + solve_sems()
        + [pltpu.SemaphoreType.DMA((n,)) for n in (1, 4, 4, 4, 8, 2, 2, 2)]
        + [pltpu.SMEM((1, 1), jnp.int32), pltpu.SMEM((1, 1), F32), pltpu.SMEM((1, 2), jnp.int32)]
        + [pltpu.VMEM((72, 128), BF16), pltpu.VMEM((24, 128), BF16), pltpu.VMEM((4, 128), jnp.int32), pltpu.VMEM((9, 8, 128), F32)],
        compiler_params=pltpu.CompilerParams(collective_id=0, has_side_effects=True, vmem_limit_bytes=60 * 2**20),
        name="reduced_system",
    )(
        pair_points.reshape(1, 1), damping.reshape(1, 1), pair_groups, jac_camera[0].reshape(72, 128), jac_point[0].reshape(24, 128), obs_camera[0],
        rhs.transpose(1, 0, 2),
    )
    tile, solved = pl.pallas_call(
        hand_over,
        out_shape=(jax.ShapeDtypeStruct((72, 2304), F32), jax.ShapeDtypeStruct((9, 8, 128), F32)),
        in_specs=[far] * 2,
        out_specs=(far, far),
        scratch_shapes=[pltpu.VMEM((72, 2304), F32), pltpu.VMEM((9, 8, 128), F32), pltpu.SemaphoreType.DMA((2, 4))],
        compiler_params=pltpu.CompilerParams(vmem_limit_bytes=60 * 2**20),
        name="hand_over",
    )(tile, solved)
    return tile[None], solved.transpose(1, 0, 2)


def solution(mesh):
    placed = (P("cam", None, None, "pts"), P("cam", None, None, "pts"), P("cam", None, "pts"), P("cam", None), P("cam"), P(), P())
    return jax.shard_map(body, mesh=mesh, in_specs=placed, out_specs=(P("cam", "pts", None), P()), check_vma=False)
```

```python
import functools
import jax
import jax.numpy as jnp
from jax import lax
from jax.experimental import pallas as pl
from jax.experimental.pallas import tpu as pltpu
from jax.sharding import PartitionSpec as P

F32 = jnp.float32
BF16 = jnp.bfloat16
ROWS = 112
XROWS = 104
UNROLL = 4


def iota(shape, dim):
    return lax.broadcasted_iota(jnp.int32, shape, dim)


def sym(a, b):
    return (a, b) if a <= b else (b, a)


def rounded(value):
    return value.astype(BF16).astype(F32)


def geometry(load, damp):
    jp = {(r, j, k): load(72 + (3 * r + j) * 4 + k) for r in range(2) for j in range(3) for k in range(4)}
    normal = {}
    for a in range(3):
        for b in range(a, 3):
            total = None
            for k in range(4):
                for r in range(2):
                    term = jp[r, a, k] * jp[r, b, k]
                    total = term if total is None else total + term
            normal[a, b] = total + damp if a == b else total
    n00, n01, n02 = normal[0, 0], normal[0, 1], normal[0, 2]
    n11, n12, n22 = normal[1, 1], normal[1, 2], normal[2, 2]
    c00 = n11 * n22 - n12 * n12
    c01 = n02 * n12 - n01 * n22
    c02 = n01 * n12 - n02 * n11
    c11 = n00 * n22 - n02 * n02
    c12 = n01 * n02 - n00 * n12
    c22 = n00 * n11 - n01 * n01
    scale = 1.0 / (n00 * c00 + n01 * c01 + n02 * c02)
    inv = {(0, 0): c00 * scale, (0, 1): c01 * scale, (0, 2): c02 * scale,
           (1, 1): c11 * scale, (1, 2): c12 * scale, (2, 2): c22 * scale}
    weighted = {}
    for k in range(4):
        for r in range(2):
            for l in range(3):
                weighted[r, k, l] = sum(jp[r, j, k] * inv[sym(j, l)] for j in range(1, 3)) + jp[r, 0, k] * inv[sym(0, l)]
    reduced = {}
    for a in range(8):
        for b in range(a, 8):
            k, r, m, s = a // 2, a % 2, b // 2, b % 2
            value = weighted[r, k, 0] * jp[s, 0, m] + weighted[r, k, 1] * jp[s, 1, m] + weighted[r, k, 2] * jp[s, 2, m]
            reduced[a, b] = 1.0 - value if a == b else -value

    def red(k, r, m, s):
        return reduced[sym(2 * k + r, 2 * m + s)]

    return red


def own_diagonal(x_ref, dg_ref, damp):
    def load(q):
        return x_ref[pl.ds(q, 1), :]

    red = geometry(load, damp)
    for m in range(4):
        for j in range(9):
            jac = [load((9 * r + j) * 4 + m) for r in range(2)]
            parts = [rounded(jac[0] * red(m, 0, m, s) + jac[1] * red(m, 1, m, s)) * jac[s] for s in range(2)]
            dg_ref[pl.ds(m * 16 + j, 1), :] = parts[0] + parts[1]


def point_blocks(x_ref, b_ref, b8_ref, slot_ref, damp, live, i_low, i_high):
    def load(q):
        return x_ref[pl.ds(q, 8, stride=XROWS), :]

    for k in range(4):
        slot_ref[pl.ds(k * 8, 8), :] = jnp.where(live, load(96 + k), -1.0)
    red = geometry(load, damp)

    def camera(r, i, k):
        return load((9 * r + i) * 4 + k)

    for m in range(4):
        right = {(s, j): camera(s, j, m) for s in range(2) for j in range(9)}
        for k in range(4):
            for which, i in enumerate((i_low, i_high)):
                left = [camera(r, i, k) for r in range(2)]
                mixed = [
                    rounded(left[0] * red(k, 0, m, s) + left[1] * red(k, 1, m, s)) for s in range(2)
                ]
                base = (which * 16 + k * 4 + m)
                for j in range(9):
                    value = mixed[0] * right[0, j] + mixed[1] * right[1, j]
                    if j < 8:
                        b_ref[pl.ds(base * 64 + j, 8, stride=8), :] = value
                    else:
                        b8_ref[pl.ds(base * 8, 8), :] = value


def twice(value):
    return jnp.concatenate([value, value], axis=0).astype(BF16)


def spread_row(ref, index):
    return jnp.broadcast_to(ref[pl.ds(index, 1), :], (8, 128))


def push_places(s, register, slot_ref, iota_ref):
    slots = [twice(spread_row(slot_ref, k * 8 + s)) for k in range(4)]
    zero = jnp.zeros((16, 128), BF16)
    one = jnp.ones((16, 128), BF16)
    places = [iota_ref[pl.ds(b * 16, 16), :] for b in range(16)]
    for unit in range(2):
        columns = [
            jnp.concatenate([jnp.where(slots[m] == value, one, zero) for value in places], axis=0)
            for m in (2 * unit, 2 * unit + 1)
        ]
        pltpu.matmul_push_rhs(jnp.concatenate(columns, axis=1), register, unit, transpose=True)
    return slots


def build_source(s, register, slots, accs, pb_ref, b_ref, b8_ref, target_ref, target8_ref, which_i):
    row = spread_row
    zero = jnp.zeros((16, 128), BF16)
    for which in range(2):
        for km in range(16):
            base = pl.multiple_of(((which * 16 + km) * 8 + s) * 8, 8)
            pb_ref[which, pl.ds(km * 16, 16), :] = twice(b_ref[pl.ds(base, 8), :])

    def choose(masks, values):
        value = zero
        for k in range(4):
            value = jnp.where(masks[k], values[k], value)
        return value

    def feed(block, parts):
        for unit in range(2):
            left = jnp.concatenate([parts[2 * unit], parts[2 * unit + 1]], axis=1)
            pltpu.matmul_acc_lhs(accs[unit][block], left, load_staged_rhs=register if block == 0 else None)

    for g in range(9):
        which = which_i[g]
        ops = [pb_ref[which, pl.ds(km * 16, 16), :] for km in range(16)]
        for b in range(4):
            target = target_ref[pl.ds((g * 4 + b) * 16, 16), :]
            masks = [slots[k] == target for k in range(4)]
            feed(g * 4 + b, [choose(masks, [ops[k * 4 + m] for k in range(4)]) for m in range(4)])
    for b in range(5):
        target = target8_ref[pl.ds(b * 16, 16), :]
        masks = [slots[k] == target for k in range(4)]
        low, high = which_i[2 * b], which_i[min(2 * b + 1, 8)]
        parts = []
        for m in range(4):
            values = []
            for k in range(4):
                km = k * 4 + m
                both = jnp.concatenate(
                    [row(b8_ref, (low * 16 + km) * 8 + s), row(b8_ref, (high * 16 + km) * 8 + s)], axis=0
                )
                values.append(both.astype(BF16))
            parts.append(choose(masks, values))
        feed(36 + b, parts)


def place(position):
    first_row = position * 72
    half = position // 16
    inside = first_row - half * 1152
    i_low = inside // 128
    start = inside - i_low * 128
    i_high = jnp.minimum(i_low + 1, 8)
    which_i = [(start + 8 * g) // 128 for g in range(9)]
    return half, start, i_low, i_high, which_i


def prepare(position, scr):
    dg_ref, target_ref, target8_ref, iota_ref = scr[3], scr[6], scr[7], scr[8]
    half, start, _, _, _ = place(position)

    def slot_of(r):
        return half * 128 + (start + r) % 128

    target_ref[...] = slot_of(iota((576, 128), 0) // 8).astype(F32).astype(BF16)
    row8 = iota((80, 128), 0)
    target8_ref[...] = jnp.where(row8 < 72, slot_of(row8), -2).astype(F32).astype(BF16)
    iota_ref[...] = iota((256, 128), 0).astype(F32).astype(BF16)
    dg_ref[...] = jnp.zeros_like(dg_ref)


def make_group(read_chunk, count, damp, position, scr, accs):
    (x_ref, b_ref, b8_ref, _, slot_ref, pb_ref, target_ref, target8_ref, iota_ref) = scr
    accs = (accs[:41], accs[41:])
    _, _, i_low, i_high, which_i = place(position)

    def group(row):
        def widen(s, carry):
            x_ref[pl.ds(pl.multiple_of(s * XROWS, 8), XROWS), :] = read_chunk(row * 8 + s)[:XROWS].astype(F32)
            return carry

        lax.fori_loop(0, 8, widen, 0)
        sub = iota((8, 128), 0)
        index = ((row * 4 + sub % 4) * 2 + sub // 4) * 128 + iota((8, 128), 1)
        point_blocks(x_ref, b_ref, b8_ref, slot_ref, damp, index < count, i_low, i_high)

        def sources(t, carry):
            first = t * UNROLL
            slots = {}
            for u in range(min(2, UNROLL)):
                slots[u] = push_places(first + u, u % 2, slot_ref, iota_ref)
            for u in range(UNROLL):
                build_source(
                    first + u, u % 2, slots[u], accs, pb_ref.at[u], b_ref, b8_ref, target_ref, target8_ref, which_i
                )
                if u + 2 < UNROLL:
                    slots[u + 2] = push_places(first + u + 2, u % 2, slot_ref, iota_ref)
            return carry

        lax.fori_loop(0, 8 // UNROLL, sources, 0)

    def finish(acc_ref):
        for block in range(41):
            value = pltpu.matmul_pop(accs[0][block]) + pltpu.matmul_pop(accs[1][block])
            for h in range(2):
                acc_ref[h, pl.ds(block * 16, 16), :] = value[:, h * 128 : h * 128 + 128]

    return group, finish


def scratch():
    return [
        pltpu.VMEM((8 * XROWS, 128), F32),
        pltpu.VMEM((2 * 16 * 64, 128), F32),
        pltpu.VMEM((2 * 16 * 8, 128), F32),
        pltpu.VMEM((64, 128), F32),
        pltpu.VMEM((4 * 8, 128), F32),
        pltpu.VMEM((UNROLL, 2, 256, 128), BF16),
        pltpu.VMEM((576, 128), BF16),
        pltpu.VMEM((80, 128), BF16),
        pltpu.VMEM((256, 128), BF16),
    ]


def accumulators():
    return [pltpu.ACC(unit)((16, 256), F32) for unit in range(2) for _ in range(41)]


def unpack_tile(acc_ref, tile_ref):
    def one(g, carry):
        rows = pl.ds(pl.multiple_of(g * 8, 8), 8)
        for h in range(2):
            for j in range(8):
                tile_ref[rows, pl.ds(h * 1152 + j * 128, 128)] = acc_ref[h, pl.ds(g * 64 + j, 8, stride=8), :]
            tile_ref[rows, pl.ds(h * 1152 + 1024, 128)] = acc_ref[h, pl.ds(pl.multiple_of(576 + g * 8, 8), 8), :]
        return carry

    lax.fori_loop(0, 9, one, 0)


MESH = pl.DeviceIdType.MESH
PTS = 32
CAM = 8


def here():
    return lax.axis_index("pts"), lax.axis_index("cam")


def plane_peer(d):
    pts, cam = here()
    return (pts + d) % PTS, cam


def line_peer(d):
    pts, cam = here()
    return pts, (cam + d) % CAM


def greet(plane, line):
    barrier = pltpu.get_barrier_semaphore()
    if plane:
        def one(d, carry):
            pl.semaphore_signal(barrier, inc=1, device_id=plane_peer(d), device_id_type=MESH)
            return carry

        lax.fori_loop(1, PTS, one, 0)
    if line:
        for d in range(1, CAM):
            pl.semaphore_signal(barrier, inc=1, device_id=line_peer(d), device_id_type=MESH)


def greeted(plane, line):
    pl.semaphore_wait(pltpu.get_barrier_semaphore(), (PTS - 1 if plane else 0) + (CAM - 1 if line else 0))


class Exchange:
    def __init__(self, plane, blocks, sem):
        self.size = PTS if plane else CAM
        self.peer = plane_peer if plane else line_peer
        self.me = here()[0 if plane else 1]
        self.blocks, self.sem = blocks, sem

    def copy(self, d):
        own = self.blocks(self.me, 1)
        return pltpu.make_async_remote_copy(
            src_ref=own, dst_ref=own, send_sem=self.sem.at[0], recv_sem=self.sem.at[1],
            device_id=self.peer(d), device_id_type=MESH,
        )

    def all_others(self):
        others = self.blocks(0, self.size - 1)
        return pltpu.make_async_remote_copy(
            src_ref=others, dst_ref=others, send_sem=self.sem.at[0], recv_sem=self.sem.at[1],
            device_id=self.peer(1), device_id_type=MESH,
        )

    def send(self):
        def one(d, carry):
            self.copy(d).start()
            return carry

        lax.fori_loop(1, self.size, one, 0)

    def receive(self):
        self.all_others().wait_recv()

    def sent(self):
        self.all_others().wait_send()


def blocks_of(ref, rows):
    return lambda first, count: ref.at[pl.ds(first * rows if isinstance(first, int) else pl.multiple_of(first * rows, rows), count * rows), :]


def pos_place(position):
    first_row = position * 72
    half = position // 16
    inside = first_row % 1152
    return half, inside // 128, inside % 128


def spread(ref, index):
    return jnp.broadcast_to(ref[pl.ds(index, 1), :], (8, 128))


def total_of(values):
    total = values[0]
    for value in values[1:]:
        total = total + value
    return jnp.sum(jnp.sum(total, axis=0, keepdims=True), axis=1, keepdims=True)


def by_group(zd_ref, half, value):
    groups = iota((8, 128), 0).astype(F32)
    total = jnp.zeros((8, 128), F32)
    for t in range(CAM):
        total = total + jnp.where(spread(zd_ref, t * 8 + 1 + half) == groups, value(t), 0.0)
    return total


def solve(tile_ref, groups_ref, damp, rhs_ref, out_ref, zd_ref, pd_ref, v_ref, zq_ref, pq_ref, zs_ref, ps_ref, pd, sems, meanwhile, settle):
    position, cam = here()
    half, start, i_low, i_high, which_i = place(position)
    group_of = [groups_ref[0, 0], groups_ref[0, 1]]
    sub = iota((8, 128), 0)
    lane = iota((8, 128), 1)
    meanwhile()
    pd.receive()

    def assemble(ref, base):
        sums = list(base)
        for p in range(PTS):
            _, low, first = pos_place(p)
            value = ref[pl.ds(p * 8, 8), :]
            if first + 72 > 128:
                sums[low] = sums[low] + jnp.where(lane >= first, value, 0.0)
                sums[low + 1] = sums[low + 1] + jnp.where(lane >= first, 0.0, value)
            else:
                sums[low] = sums[low] + value
        return sums

    residual = [rhs_ref[i] for i in range(9)]
    diagonal = assemble(pd_ref, [jnp.full((8, 128), damp, F32)] * 9)
    precond = [residual[i] / diagonal[i] for i in range(9)]
    inner = total_of([residual[i] * precond[i] for i in range(9)])
    def image_row(vector):
        for i in range(9):
            v_ref[pl.ds(i * 8, 8), :] = vector[i]
        ops = [[spread(v_ref, j * 8 + group_of[h]) for j in range(9)] for h in range(2)]
        placed = jnp.zeros((8, 128), F32)
        for g in range(9):
            total = None
            for h in range(2):
                for j in range(9):
                    term = tile_ref[pl.ds(g * 8, 8), pl.ds((h * 9 + j) * 128, 128)] * ops[h][j]
                    total = term if total is None else total + term
            value = jnp.sum(total, axis=1, keepdims=True)
            placed = placed + jnp.where(lane == (start + 8 * g + sub) % 128, value, 0.0)
        return jnp.sum(placed, axis=0, keepdims=True)

    zq_ref[pl.ds(cam, 1), :] = image_row(precond)
    zq = Exchange(False, blocks_of(zq_ref, 1), sems[0])
    zq.send()
    zq.receive()
    total = by_group(zd_ref, half, lambda t: spread(zq_ref, t))
    pq_ref[pl.ds(pl.multiple_of(position * 8, 8), 8), :] = total
    pq = Exchange(True, blocks_of(pq_ref, 8), sems[1])
    pq.send()
    pq.receive()
    image = assemble(pq_ref, [damp * precond[i] for i in range(9)])
    alpha = inner / total_of([precond[i] * image[i] for i in range(9)])
    residual = [residual[i] - alpha * image[i] for i in range(9)]
    scaled = [residual[i] / diagonal[i] for i in range(9)]
    inner_next = total_of([residual[i] * scaled[i] for i in range(9)])
    beta = inner_next / inner
    direction = [scaled[i] + beta * precond[i] for i in range(9)]
    row = image_row(direction)
    own_group = jnp.where(half == 0, group_of[0], group_of[1])
    lane_row = iota((1, 128), 1)
    own = jnp.where(
        lane_row >= start, v_ref[pl.ds(i_low * 8 + own_group, 1), :], v_ref[pl.ds(i_high * 8 + own_group, 1), :]
    )
    zs_ref[pl.ds(cam, 1), :] = row * own
    zs = Exchange(False, blocks_of(zs_ref, 1), sems[2])
    zs.send()
    for exchange in (pd, zq, pq):
        exchange.sent()
    settle()
    zs.receive()
    ps_ref[pl.ds(position, 1), :] = jnp.sum(zs_ref[...], axis=0, keepdims=True)
    ps = Exchange(True, blocks_of(ps_ref, 1), sems[3])
    ps.send()
    ps.receive()
    curvature = damp * total_of([value * value for value in direction]) + total_of(
        [ps_ref[pl.ds(8 * n, 8), :] for n in range(4)]
    )
    second = inner_next / curvature
    for i in range(9):
        out_ref[i] = alpha * precond[i] + second * direction[i]
    zs.sent()
    ps.sent()


def solve_scratch():
    return [
        pltpu.VMEM((CAM * 8, 128), F32),
        pltpu.VMEM((PTS * 8, 128), F32),
        pltpu.VMEM((72, 128), F32),
        pltpu.VMEM((CAM, 128), F32),
        pltpu.VMEM((PTS * 8, 128), F32),
        pltpu.VMEM((CAM, 128), F32),
        pltpu.VMEM((PTS, 128), F32),
    ]


def solve_sems():
    return [pltpu.SemaphoreType.DMA((2,)) for _ in range(4)]


def near_offsets():
    return [(0, dx, dc) for dc in range(2) for dx in range(4) if (dx, dc) != (0, 0)]


def far_offsets():
    return [(dy, dx, 0) for dy in (3, 2, 1) for dx in range(4)]


def partial_diagonal(x_ref, dg_ref, position, count, damp, part_ref, rows_out):
    own_diagonal(x_ref, dg_ref, damp)
    lane = iota((1, 128), 1)
    live = position * 128 + lane < count
    places = iota((256, 128), 0).astype(F32)
    left, right = [], []
    for k in range(4):
        slot = jnp.where(live, x_ref[pl.ds(96 + k, 1), :], -1.0)
        left.append(dg_ref[pl.ds(k * 16, 16), :].astype(BF16))
        right.append((jnp.broadcast_to(slot, (256, 128)) == places).astype(F32).astype(BF16))

    def product(*accs):
        for unit in range(2):
            pair = (2 * unit, 2 * unit + 1)
            pltpu.matmul_push_rhs(jnp.concatenate([right[k] for k in pair], axis=1), 0, unit, transpose=True)
            pltpu.matmul_acc_lhs(accs[unit], jnp.concatenate([left[k] for k in pair], axis=1), load_staged_rhs=0)
        value = pltpu.matmul_pop(accs[0]) + pltpu.matmul_pop(accs[1])
        for h in range(2):
            part_ref[h] = value[:, h * 128 : h * 128 + 128]

    pl.run_scoped(product, *[pltpu.ACC(unit)((16, 256), F32) for unit in range(2)])
    for p in range(PTS):
        h, low, first = pos_place(p)
        row = part_ref[h, low : low + 1, :]
        if first + 72 > 128:
            row = jnp.where(lane >= first, row, part_ref[h, low + 1 : low + 2, :])
        rows_out[p : p + 1, :] = row


def whole_kernel(count_in, damp_in, groups_in, camera_in, point_in, obs_in, rhs_in, tile_out, out_ref, gbuf, tile_ref, acc_ref, part_ref, rows_out, rows_in, *scr):
    work, rest = scr[:9], scr[9:]
    vectors, rest = rest[:7], rest[7:]
    sems, rest = rest[:4], rest[4:]
    send_sem, recv_sem, share_send, share_recv, load_sem, row_sem, zd_sem, pd_sem = rest[:8]
    count_ref, damp_ref, groups_ref, camera_ref, point_ref, obs_ref, rhs_ref = rest[8:]
    position, cam = here()
    y, x, c = position // 8, position // 2 % 4, position % 2
    inputs = (count_in, damp_in, groups_in, camera_in, point_in, obs_in, rhs_in)
    loads = [pltpu.make_async_copy(src, dst, load_sem.at[n]) for n, (src, dst) in enumerate(zip(inputs, rest[8:]))]
    for load in loads:
        load.start()
    greet(True, True)
    prepare(position, work)
    for load in loads:
        load.wait()
    cameras = obs_ref[...]
    slot = jnp.where(cameras // 128 == groups_ref[0, 1], 128, 0) + cameras % 128
    chunk = jnp.concatenate(
        [camera_ref[...].astype(F32), point_ref[...].astype(F32), slot.astype(F32), jnp.zeros((12, 128), F32)], axis=0
    )
    gbuf[(y * 2 + c) * 4 + x] = chunk.astype(BF16)
    damp = damp_ref[0, 0]
    half, start, _, _, _ = place(position)
    x_ref, dg_ref = work[0], work[3]
    x_ref[pl.ds(0, XROWS), :] = chunk[:XROWS]
    partial_diagonal(x_ref, dg_ref, position, count_ref[0, 0], damp, part_ref, rows_out)
    rows_in[pl.ds(position, 1), :] = rows_out[pl.ds(position, 1), :]
    greeted(True, True)

    def spread_copy(dy, dx, dc):
        own = gbuf.at[(y * 2 + c) * 4 + x]
        other = ((y + dy) % 4 * 4 + (x + dx) % 4) * 2 + (c + dc) % 2
        return pltpu.make_async_remote_copy(
            src_ref=own, dst_ref=own, send_sem=send_sem.at[0], recv_sem=recv_sem.at[y],
            device_id=(other, cam), device_id_type=MESH,
        )

    def chunks(first, count):
        where = gbuf.at[pl.ds(first, count)]
        return lambda send, recv: pltpu.make_async_remote_copy(
            src_ref=where, dst_ref=where, send_sem=send, recv_sem=recv,
            device_id=(position + 1 - 2 * c, cam), device_id_type=MESH,
        )

    def share(row, core):
        return chunks((row * 2 + core) * 4, 4)(share_send.at[row], share_recv.at[row])

    for offset in near_offsets():
        spread_copy(*offset).start()

    def row_copy(d):
        other, _ = plane_peer(d)
        return pltpu.make_async_remote_copy(
            src_ref=rows_out.at[pl.ds(other, 1), :], dst_ref=rows_in.at[pl.ds(position, 1), :],
            send_sem=row_sem.at[0], recv_sem=row_sem.at[1], device_id=(other, cam), device_id_type=MESH,
        )

    def send_row(d, carry):
        row_copy(d).start()
        return carry

    lax.fori_loop(1, PTS, send_row, 0)
    for offset in far_offsets():
        spread_copy(*offset).start()

    def all_rows():
        return pltpu.make_async_remote_copy(
            src_ref=rows_out.at[pl.ds(0, PTS - 1), :], dst_ref=rows_in.at[pl.ds(0, PTS - 1), :],
            send_sem=row_sem.at[0], recv_sem=row_sem.at[1], device_id=plane_peer(1), device_id_type=MESH,
        )

    zd_ref, pd_ref = vectors[:2]
    zd = Exchange(False, blocks_of(zd_ref, 8), zd_sem)
    pd = Exchange(True, blocks_of(pd_ref, 8), pd_sem)

    def diagonal_rows():
        all_rows().wait_recv()
        own = jnp.sum(rows_in[...], axis=0, keepdims=True)
        sub = iota((8, 128), 0)
        mine = (iota((8, 128), 1) - start + 128) % 128 < 72
        first, second = groups_ref[0, 0].astype(F32), groups_ref[0, 1].astype(F32)
        value = jnp.where(sub == 0, jnp.where(mine, own, 0.0), jnp.where(sub == 1, first, second))
        zd_ref[pl.ds(pl.multiple_of(cam * 8, 8), 8), :] = value
        zd.send()

    def diagonal_groups():
        zd.receive()
        pd_ref[pl.ds(pl.multiple_of(position * 8, 8), 8), :] = by_group(zd_ref, half, lambda t: spread(zd_ref, t * 8))
        pd.send()

    def hand_on(row):
        chunks((row * 2 + c) * 4, 4)(send_sem.at[0], recv_sem.at[row]).wait_recv()
        share(row, c).start()

    def assemble(*accs):
        group, finish = make_group(lambda s: gbuf[s], count_ref[0, 0], damp, position, work, accs)
        diagonal_rows()
        chunks(y * 8, 7)(send_sem.at[0], recv_sem.at[y]).wait_recv()
        hand_on((y + 1) % 4)

        def one(step, carry):
            row = (y + step) % 4

            @pl.when(step > 0)
            def _():
                share(row, 1 - c).wait_recv()

            group(row)

            @pl.when(step == 0)
            def _():
                hand_on((y + 2) % 4)

            @pl.when(step == 1)
            def _():
                hand_on((y + 3) % 4)
                diagonal_groups()

            return carry

        lax.fori_loop(0, 4, one, 0)
        finish(acc_ref)

    pl.run_scoped(assemble, *accumulators())
    store = pltpu.make_async_copy(tile_ref, tile_out, load_sem.at[7])

    def unpack():
        unpack_tile(acc_ref, tile_ref)
        store.start()

    def settle():
        store.wait()
        all_rows().wait_send()
        zd.sent()
        chunks(0, 19)(send_sem.at[0], recv_sem.at[0]).wait_send()
        for step in range(1, 4):
            share((y + step) % 4, c).wait_send()

    solve(
        tile_ref, groups_ref, damp, rhs_ref, out_ref, *vectors, pd, sems,
        unpack, settle,
    )


def hand_over(tile_in, solved_in, tile_out, solved_out, tile_buf, solved_buf, sem):
    pieces = [pl.ds(24 * n, 24) for n in range(3)]
    stages = [(tile_in.at[p, :], tile_buf.at[p, :], tile_out.at[p, :]) for p in pieces] + [(solved_in, solved_buf, solved_out)]
    loads = [pltpu.make_async_copy(src, buf, sem.at[0, n]) for n, (src, buf, _) in enumerate(stages)]
    stores = [pltpu.make_async_copy(buf, dst, sem.at[1, n]) for n, (_, buf, dst) in enumerate(stages)]
    for load in loads:
        load.start()
    for load, store in zip(loads, stores):
        load.wait()
        store.start()
    for store in stores:
        store.wait()


def body(jac_camera, jac_point, obs_camera, pair_groups, pair_points, damping, rhs):
    vm = pl.BlockSpec(memory_space=pltpu.VMEM)
    far = pl.BlockSpec(memory_space=pltpu.HBM)
    tile, solved = pl.pallas_call(
        whole_kernel,
        out_shape=(jax.ShapeDtypeStruct((72, 2304), F32), jax.ShapeDtypeStruct((9, 8, 128), F32)),
        in_specs=[far] * 7,
        out_specs=(far, vm),
        scratch_shapes=[pltpu.VMEM((PTS, ROWS, 128), BF16), pltpu.VMEM((72, 2304), F32), pltpu.VMEM((2, 656, 128), F32), pltpu.VMEM((2, 16, 128), F32)]
        + [pltpu.VMEM((PTS, 128), F32), pltpu.VMEM((PTS, 128), F32)]
        + scratch()
        + solve_scratch()
        + solve_sems()
        + [pltpu.SemaphoreType.DMA((n,)) for n in (1, 4, 4, 4, 8, 2, 2, 2)]
        + [pltpu.SMEM((1, 1), jnp.int32), pltpu.SMEM((1, 1), F32), pltpu.SMEM((1, 2), jnp.int32)]
        + [pltpu.VMEM((72, 128), BF16), pltpu.VMEM((24, 128), BF16), pltpu.VMEM((4, 128), jnp.int32), pltpu.VMEM((9, 8, 128), F32)],
        compiler_params=pltpu.CompilerParams(collective_id=0, has_side_effects=True, vmem_limit_bytes=60 * 2**20),
        name="reduced_system",
    )(
        pair_points.reshape(1, 1), damping.reshape(1, 1), pair_groups, jac_camera[0].reshape(72, 128), jac_point[0].reshape(24, 128), obs_camera[0],
        rhs.transpose(1, 0, 2),
    )
    tile, solved = pl.pallas_call(
        hand_over,
        out_shape=(jax.ShapeDtypeStruct((72, 2304), F32), jax.ShapeDtypeStruct((9, 8, 128), F32)),
        in_specs=[far] * 2,
        out_specs=(far, far),
        scratch_shapes=[pltpu.VMEM((72, 2304), F32), pltpu.VMEM((9, 8, 128), F32), pltpu.SemaphoreType.DMA((2, 4))],
        compiler_params=pltpu.CompilerParams(vmem_limit_bytes=60 * 2**20),
        name="hand_over",
    )(tile, solved)
    return tile[None], solved.transpose(1, 0, 2)


def solution(mesh):
    placed = (P("cam", None, None, "pts"), P("cam", None, None, "pts"), P("cam", None, "pts"), P("cam", None), P("cam"), P(), P())
    return jax.shard_map(body, mesh=mesh, in_specs=placed, out_specs=(P("cam", "pts", None), P()), check_vma=False)
```
